256 devices in a mesh: patch: 32 (over y_hi, z, core), tp: 8 (over y_lo, x).
Axes of the slice: x: 4, y: 4 (y_hi: 2, y_lo: 2; y = y_hi * 2 + y_lo), z: 8, core: 2. Of those that a mesh axis runs over, the one named last changes fastest.
Arguments:
- image: bfloat16 [6144, 3072], P('patch'), may hold values from -1.5 to 1.5
- mod_shift: float32 [3072], replicated, may hold values from -3 to 3
- mod_scale: float32 [3072], replicated, may hold values from -3 to 3
- mod_gate: float32 [3072], replicated, may hold values from -6 to 6
- qkv_weight: bfloat16 [3072, 3, 2048], P(None, None, 'tp'), may hold values from -0.109375 to 0.109375
- qkv_bias: float32 [3, 2048], P(None, 'tp'), may hold values from -3 to 3
- q_gain: float32 [128], replicated, may hold values from 1 to 2.5
- k_gain: float32 [128], replicated, may hold values from 1 to 2.5
- stale_kv: bfloat16 [2, 6144, 2048], P(None, 'patch', 'tp'), may hold values from -2.5 to 2.5
- text_kv: bfloat16 [2, 512, 2048], P(None, None, 'tp'), may hold values from -2.5 to 2.5
- out_weight: bfloat16 [2048, 3072], P('tp'), may hold values from -1 to 1
- out_bias: float32 [3072], replicated, may hold values from -3 to 3
Outputs:
- mixed: bfloat16 [6144, 3072], P('patch')
- fresh_kv: bfloat16 [2, 6144, 2048], P(None, 'patch', 'tp')
The draws below stay inside these ranges and needn't reach their ends.
All inputs are finite; a program needn't handle non-finite values.
Results may differ from the reference program's by a relative error of at most 0.0098.
Values may be sent and summed in bfloat16 or wider, within the bound.
No kernel may reach another device: no remote copies, remote signals or barrier semaphores. Data moves between devices by JAX's collectives and lax.ppermute only.
A program may use at most 128 MiB of HBM per device.

```python
import math
import jax
import jax.numpy as jnp
from jax import lax

D = 3072
HEADS = 16
HD = 128
TXT = 512
TOK_DEV = 192
TOKENS = 6144


def shard_levels(rng, shape, shards, least, top_value):
    factor_of = 1.0
    for position, blocks in shards:
        heights = jax.random.uniform(jax.random.fold_in(jax.random.fold_in(rng, 6), position), (blocks,), jnp.float32, least / len(shards), top_value / len(shards))
        factor_of = factor_of * jnp.repeat(jnp.exp(heights), shape[position] // blocks).reshape((-1,) + (1,) * (len(shape) - 1 - position))
    return factor_of


def gaussian(stream_key, shape, deviation, limit, cuts=(), held_as=jnp.bfloat16):
    level = shard_levels(stream_key, shape, cuts, -0.22, 0.18) if cuts else 1.0
    entries = jax.random.normal(stream_key, shape, jnp.float32) * deviation * level
    return jnp.minimum(jnp.maximum(entries, -limit), limit).astype(held_as)


def setup_inputs(seed: int = 0) -> dict:
    arg_keys = jax.random.split(jax.random.key(seed), 13)
    return {
        "image": gaussian(arg_keys[0], (TOKENS, D), 0.25, 1.5, ((0, 32),)),
        "mod_shift": gaussian(arg_keys[1], (D,), 0.5, 3.0, (), jnp.float32),
        "mod_scale": gaussian(arg_keys[2], (D,), 0.5, 3.0, (), jnp.float32),
        "mod_gate": gaussian(arg_keys[3], (D,), 1.0, 6.0, (), jnp.float32),
        "qkv_weight": gaussian(arg_keys[4], (D, 3, HEADS * HD), D ** -0.5, 0.109375, ((2, 8),)),
        "qkv_bias": gaussian(arg_keys[5], (3, HEADS * HD), 0.5, 3.0, ((1, 8),), jnp.float32),
        "q_gain": jnp.clip(jax.random.uniform(arg_keys[6], (HD,), jnp.float32, 1.0, 2.5), 1.0, 2.5),
        "k_gain": jnp.clip(jax.random.uniform(arg_keys[7], (HD,), jnp.float32, 1.0, 2.5), 1.0, 2.5),
        "stale_kv": gaussian(arg_keys[8], (2, TOKENS, HEADS * HD), 1.0, 2.5, ((1, 32), (2, 8))),
        "text_kv": gaussian(arg_keys[9], (2, TXT, HEADS * HD), 1.0, 2.5, ((2, 8),)),
        "out_weight": gaussian(arg_keys[10], (HEADS * HD, D), (HD // 4) ** -0.5, 1.0, ((0, 8),)),
        "out_bias": gaussian(arg_keys[11], (D,), 0.5, 3.0, (), jnp.float32),
    }


def modulate(image, mod_shift, mod_scale):
    wide = image.astype(jnp.float32)
    average = lax.optimization_barrier(jnp.mean(wide, -1, keepdims=True))
    centred = wide - average
    spread = lax.optimization_barrier(jnp.mean(centred * centred, -1, keepdims=True))
    normed = centred * lax.rsqrt(spread + 1e-06)
    return (normed * (1.0 + mod_scale) + mod_shift).astype(jnp.bfloat16)

def head_norm(part, gain):
    tok_rows = part.shape[0]
    per_head = part.reshape(tok_rows, -1, gain.shape[0])
    scaled = per_head * lax.rsqrt(lax.optimization_barrier(jnp.mean(per_head * per_head, -1, keepdims=True)) + 1e-06) * gain
    return scaled.reshape(tok_rows, -1).astype(jnp.bfloat16)

def project(modulated, qkv_weight, qkv_bias, q_gain, k_gain):
    width = qkv_weight.shape[2]
    projected = jnp.dot(modulated, qkv_weight.reshape(qkv_weight.shape[0], 3 * width), preferred_element_type=jnp.float32)
    projected = projected.reshape(-1, 3, width) + qkv_bias
    queries = head_norm(projected[:, 0], q_gain)
    keys = head_norm(projected[:, 1], k_gain)
    values = projected[:, 2].astype(jnp.bfloat16)
    return (queries, keys, values)

def attend(queries, keys, values, head_size):
    query_heads = queries.reshape(queries.shape[0], -1, head_size).astype(jnp.float32)
    key_heads = keys.reshape(keys.shape[0], -1, head_size).astype(jnp.float32)
    value_heads = values.reshape(values.shape[0], -1, head_size).astype(jnp.float32)
    scores = jnp.einsum('thd,rhd->thr', query_heads, key_heads) * (1.0 / math.sqrt(head_size))
    weights = jnp.exp(scores)
    totals = lax.optimization_barrier(jnp.sum(weights, -1))
    rounded = lax.optimization_barrier(weights.astype(jnp.bfloat16)).astype(jnp.float32)
    summed = jnp.einsum('thr,rhd->thd', rounded, value_heads)
    return (summed, totals)

def reference(image, mod_shift, mod_scale, mod_gate, qkv_weight, qkv_bias, q_gain, k_gain, stale_kv, text_kv, out_weight, out_bias):
    modulated = modulate(image, mod_shift, mod_scale)
    queries, keys, values = project(modulated, qkv_weight, qkv_bias, q_gain, k_gain)
    fresh_kv = jnp.stack([keys, values])

    def one_patch(patch_index):
        first_row = (patch_index * TOK_DEV).astype(jnp.int32)
        own_queries = lax.dynamic_slice_in_dim(queries, first_row, TOK_DEV, 0)
        own_keys = lax.dynamic_slice_in_dim(keys, first_row, TOK_DEV, 0)
        own_values = lax.dynamic_slice_in_dim(values, first_row, TOK_DEV, 0)
        all_keys = lax.dynamic_update_slice_in_dim(stale_kv[0], own_keys, first_row, 0)
        all_values = lax.dynamic_update_slice_in_dim(stale_kv[1], own_values, first_row, 0)
        all_keys = jnp.concatenate([text_kv[0], all_keys], 0)
        all_values = jnp.concatenate([text_kv[1], all_values], 0)
        summed, totals = attend(own_queries, all_keys, all_values, HD)
        return (summed / totals[..., None]).reshape(TOK_DEV, -1).astype(jnp.bfloat16)
    attended = lax.map(one_patch, jnp.arange(TOKENS // TOK_DEV, dtype=jnp.int32)).reshape(TOKENS, -1)
    projection = jnp.dot(attended, out_weight, preferred_element_type=jnp.float32) + out_bias
    mixed = (image.astype(jnp.float32) + mod_gate * projection).astype(jnp.bfloat16)
    return (mixed, fresh_kv)
```

```python
import math

import jax
import jax.numpy as jnp
from jax import lax
from jax.experimental import pallas as pl
from jax.experimental.pallas import tpu as pltpu
from jax.sharding import PartitionSpec as P

BF = jnp.bfloat16
F32 = jnp.float32
VMEM = pl.BlockSpec(memory_space=pltpu.VMEM)
LIMIT = 48 * 1024 * 1024


def params(**kw):
    return pltpu.CompilerParams(vmem_limit_bytes=LIMIT, **kw)


def modulate_into(image_ref, shift_ref, scale_ref, out_ref):
    rows = image_ref.shape[0]
    step = 16

    def body(i, carry):
        at = pl.ds(pl.multiple_of(i * step, step), step)
        wide = image_ref[at, :].astype(F32)
        average = jnp.mean(wide, -1, keepdims=True)
        centred = wide - average
        spread = jnp.mean(centred * centred, -1, keepdims=True)
        normed = centred * lax.rsqrt(spread + 1e-06)
        out_ref[at, :] = (normed * (1.0 + scale_ref[...]) + shift_ref[...]).astype(BF)
        return carry

    lax.fori_loop(0, rows // step, body, 0)


def finish_heads(acc, bias_ref, q_gain_ref, k_gain_ref, out_ref):
    hd = q_gain_ref.shape[1]

    def norm(part, gain):
        return part * lax.rsqrt(jnp.mean(part * part, -1, keepdims=True) + 1e-06) * gain

    q = acc[:, :hd] + bias_ref[0:1, :]
    k = acc[:, hd : 2 * hd] + bias_ref[1:2, :]
    v = acc[:, 2 * hd :] + bias_ref[2:3, :]
    out_ref[0] = norm(q, q_gain_ref[...]).astype(BF)
    out_ref[1] = norm(k, k_gain_ref[...]).astype(BF)
    out_ref[2] = v.astype(BF)


def own_kernel(c_ref, image_ref, shift_ref, scale_ref, w_ref, bias_ref, q_gain_ref, k_gain_ref, out_ref, wide_ref, mod_ref, acc_ref):
    k = pl.program_id(0)

    @pl.when(k == 0)
    def _():
        modulate_into(image_ref, shift_ref, scale_ref, mod_ref)
        acc_ref[...] = jnp.zeros_like(acc_ref)

    depth = w_ref.shape[0]
    flat = jnp.concatenate([w_ref[:, j, :] for j in range(3)], axis=1)
    wide_ref[...] = flat
    at = pl.ds(pl.multiple_of(k * depth, depth), depth)
    acc_ref[...] += jnp.dot(mod_ref[:, at], flat, preferred_element_type=F32)

    @pl.when(k == pl.num_programs(0) - 1)
    def _():
        finish_heads(acc_ref[...], bias_ref, q_gain_ref, k_gain_ref, out_ref)


def project_own(core, image, shift, scale, weight, bias, q_gain, k_gain):
    rows, features = image.shape
    hd = q_gain.shape[1]
    depth = features // 8
    whole = lambda shape: pl.BlockSpec(shape, lambda k, c: (0,) * len(shape))
    return pl.pallas_call(
        own_kernel,
        grid_spec=pltpu.PrefetchScalarGridSpec(
            num_scalar_prefetch=1,
            grid=(features // depth,),
            in_specs=[
                whole((rows, features)),
                whole((1, features)),
                whole((1, features)),
                pl.BlockSpec((depth, 3, hd), lambda k, c: (k, 0, c[0])),
                pl.BlockSpec((3, hd), lambda k, c: (0, c[0])),
                whole((1, hd)),
                whole((1, hd)),
            ],
            out_specs=[
                whole((3, rows, hd)),
                pl.BlockSpec((depth, 3 * hd), lambda k, c: (k, 0)),
            ],
            scratch_shapes=[
                pltpu.VMEM((rows, features), BF),
                pltpu.VMEM((rows, 3 * hd), F32),
            ],
        ),
        out_shape=[
            jax.ShapeDtypeStruct((3, rows, hd), BF),
            jax.ShapeDtypeStruct((features, 3 * hd), BF),
        ],
        compiler_params=params(),
        name="project_own",
    )(core, image, shift, scale, weight, bias, q_gain, k_gain)


def other_kernel(c_ref, image_ref, shift_ref, scale_ref, wide_ref, bias_ref, q_gain_ref, k_gain_ref, out_ref, mod_ref):
    modulate_into(image_ref, shift_ref, scale_ref, mod_ref)
    acc = jnp.dot(mod_ref[...], wide_ref[...], preferred_element_type=F32)
    finish_heads(acc, bias_ref, q_gain_ref, k_gain_ref, out_ref)


def project_other(core, image, shift, scale, wide, bias, q_gain, k_gain):
    rows, features = image.shape
    hd = q_gain.shape[1]
    whole = lambda shape: pl.BlockSpec(shape, lambda k, c: (0,) * len(shape))
    return pl.pallas_call(
        other_kernel,
        grid_spec=pltpu.PrefetchScalarGridSpec(
            num_scalar_prefetch=1,
            grid=(1,),
            in_specs=[
                whole((rows, features)),
                whole((1, features)),
                whole((1, features)),
                whole((features, 3 * hd)),
                pl.BlockSpec((3, hd), lambda k, c: (0, c[0])),
                whole((1, hd)),
                whole((1, hd)),
            ],
            out_specs=whole((3, rows, hd)),
            scratch_shapes=[pltpu.VMEM((rows, features), BF)],
        ),
        out_shape=jax.ShapeDtypeStruct((3, rows, hd), BF),
        compiler_params=params(),
        name="project_other",
    )(core, image, shift, scale, wide, bias, q_gain, k_gain)


def block_sums(q, k, v_ref_value):
    hd = q.shape[1]
    scores = lax.dot_general(q, k, (((1,), (1,)), ((), ())), preferred_element_type=F32)
    weights = jnp.exp2(scores * (math.log2(math.e) / math.sqrt(hd))).astype(BF)
    ones = jnp.ones_like(v_ref_value)
    return jnp.dot(weights, jnp.concatenate([v_ref_value, ones], 1), preferred_element_type=F32)


def eye(n):
    return (lax.broadcasted_iota(jnp.int32, (n, n), 0) == lax.broadcasted_iota(jnp.int32, (n, n), 1)).astype(F32)


def remote_kernel(q_ref, kv0_ref, kv1_ref, kv2_ref, kv3_ref, out_ref):
    rows, hd = q_ref.shape
    same = eye(hd)
    for i in range(rows // hd):
        at = slice(i * hd, (i + 1) * hd)
        q = q_ref[at, :]
        total = None
        for kv in (kv0_ref, kv1_ref, kv2_ref, kv3_ref):
            part = block_sums(q, kv[0], kv[1])
            total = part if total is None else total + part
        out_ref[at, :] = total[:, :hd].astype(BF)
        line = jnp.sum(total[:, hd:] * same, 0, keepdims=True)
        high = line.astype(BF).astype(F32)
        out_ref[pl.ds(rows + 16 * i, 16), :] = jnp.concatenate(
            [jnp.broadcast_to(high, (8, hd)), jnp.broadcast_to(line - high, (8, hd))], 0
        ).astype(BF)


def attend_remote(q, kvs):
    rows, hd = q.shape
    return pl.pallas_call(
        remote_kernel,
        in_specs=[VMEM] * 5,
        out_specs=VMEM,
        out_shape=jax.ShapeDtypeStruct((rows + 16 * (rows // hd), hd), BF),
        compiler_params=params(),
        name="attend_remote",
    )(q, *kvs)


def local_kernel(own_ref, other_ref, kv0_ref, kv1_ref, kv2_ref, kv3_ref, text_ref, out_ref):
    rows = own_ref.shape[1]
    for mine, (half, fresh) in enumerate(((0, own_ref), (1, other_ref))):
        q = fresh[0]
        stale = pl.ds((1 - half) * rows, rows)
        total = block_sums(q, fresh[1], fresh[2])
        total += block_sums(q, kv0_ref[0, stale, :], kv0_ref[1, stale, :])
        for kv in (kv1_ref, kv2_ref, kv3_ref, text_ref):
            total += block_sums(q, kv[0], kv[1])
        out_ref[pl.ds(mine * rows, rows), :] = total


def attend_local(core, own, other, kvs, text):
    _, rows, hd = own.shape
    whole = lambda a: pl.BlockSpec(a.shape, lambda k, c: (0,) * a.ndim)
    return pl.pallas_call(
        lambda c_ref, *refs: local_kernel(*refs),
        grid_spec=pltpu.PrefetchScalarGridSpec(
            num_scalar_prefetch=1,
            grid=(1,),
            in_specs=[whole(own), whole(other)]
            + [whole(kv) for kv in kvs]
            + [pl.BlockSpec((2, text.shape[1], hd), lambda k, c: (0, 0, c[0]))],
            out_specs=pl.BlockSpec((2 * rows, 2 * hd), lambda k, c: (0, 0)),
        ),
        out_shape=jax.ShapeDtypeStruct((2 * rows, 2 * hd), F32),
        compiler_params=params(),
        name="attend_local",
    )(core, own, other, *kvs, text)


def combine_kernel(local_ref, p1_ref, p2_ref, p3_ref, out_ref):
    rows, hd = out_ref.shape
    same = eye(hd)
    for i in range(rows // hd):
        at = slice(i * hd, (i + 1) * hd)
        summed = local_ref[at, :hd]
        totals = local_ref[at, hd:]
        line = None
        for p in (p1_ref, p2_ref, p3_ref):
            summed += p[at, :].astype(F32)
            pair = p[pl.ds(rows + 16 * i, 16), :].astype(F32)
            both = pair[0:1] + pair[8:9]
            line = both if line is None else line + both
        column = jnp.sum(jnp.broadcast_to(line, (hd, hd)) * same, 1, keepdims=True)
        out_ref[at, :] = (summed / (totals + column)).astype(BF)


def combine(local, parts):
    rows, hd = local.shape[0], local.shape[1] // 2
    return pl.pallas_call(
        combine_kernel,
        in_specs=[VMEM] * 4,
        out_specs=VMEM,
        out_shape=jax.ShapeDtypeStruct((rows, hd), BF),
        compiler_params=params(),
        name="combine",
    )(local, *parts)


def out_kernel(t_ref, a_ref, w_ref, image_ref, gate_ref, bias_ref, out_ref):
    n = a_ref.shape[0]
    acc = None
    for i in range(n):
        part = jnp.dot(a_ref[i], w_ref[i], preferred_element_type=F32)
        acc = part if acc is None else acc + part
    projection = acc + bias_ref[...]
    out_ref[...] = (image_ref[...].astype(F32) + gate_ref[...] * projection).astype(BF)


def project_out(tp, gathered, weight, image, gate, bias):
    n, rows, width = gathered.shape
    columns = weight.shape[2]
    return pl.pallas_call(
        out_kernel,
        grid_spec=pltpu.PrefetchScalarGridSpec(
            num_scalar_prefetch=1,
            grid=(1,),
            in_specs=[
                pl.BlockSpec((n, rows, width), lambda k, t: (0, 0, 0)),
                pl.BlockSpec((n, width, columns), lambda k, t: (0, 0, 0)),
                pl.BlockSpec((rows, columns), lambda k, t: (0, t[0])),
                pl.BlockSpec((1, columns), lambda k, t: (0, t[0])),
                pl.BlockSpec((1, columns), lambda k, t: (0, t[0])),
            ],
            out_specs=pl.BlockSpec((rows, columns), lambda k, t: (0, 0)),
        ),
        out_shape=jax.ShapeDtypeStruct((rows, columns), BF),
        compiler_params=params(),
        name="project_out",
    )(tp, gathered, weight, image, gate, bias)


def shards(image, mod_shift, mod_scale, mod_gate, qkv_weight, qkv_bias, q_gain, k_gain, stale_kv, text_kv, out_weight, out_bias):
    hd = q_gain.shape[0]
    rows, features = image.shape
    n_patch = lax.axis_size("patch")
    n_tp = lax.axis_size("tp")
    patch = lax.axis_index("patch")
    tp = lax.axis_index("tp")
    core = patch % 2
    core_at = core.astype(jnp.int32).reshape(1)
    tp_at = tp.astype(jnp.int32).reshape(1)

    def flip(bits):
        return [(i, i ^ bits) for i in range(n_patch)]

    def turn(k):
        return [(i, (i & ~12) | ((i + 4 * k) & 12)) for i in range(n_patch)]

    def send(x, perm):
        return lax.ppermute(x, "patch", perm)

    mine = lax.dynamic_slice_in_dim(stale_kv, core * hd, hd, 2)
    theirs = lax.dynamic_slice_in_dim(stale_kv, (1 - core) * hd, hd, 2)
    kv0 = jnp.concatenate([mine, send(theirs, flip(1))], 1)
    kvs = [kv0] + [send(kv0, turn(k)) for k in (1, 2, 3)]

    other_image = send(image, flip(1))
    shift = mod_shift.reshape(1, -1)
    scale = mod_scale.reshape(1, -1)
    gains = (q_gain.reshape(1, -1), k_gain.reshape(1, -1))
    own, wide = project_own(core_at, image, shift, scale, qkv_weight, qkv_bias, *gains)
    other = project_other(core_at, other_image, shift, scale, wide, qkv_bias, *gains)

    q = jnp.concatenate([own[0], other[0]], 0)
    hops = (2, 16, 18)
    partial = []
    for bits in hops:
        there = send(q, flip(bits))
        partial.append(send(attend_remote(there, kvs), flip(bits)))
    local = attend_local(core_at, own, other, kvs, text_kv)
    attended = combine(local, partial)

    back = send(other[1:], flip(1))
    first = core == 0
    fresh_kv = jnp.where(first, jnp.concatenate([own[1:], back], 2), jnp.concatenate([back, own[1:]], 2))

    swapped = send(attended[rows:], flip(1))
    kept = attended[:rows]
    heads = jnp.where(first, jnp.concatenate([kept, swapped], 1), jnp.concatenate([swapped, kept], 1))
    gathered = lax.all_to_all(jnp.broadcast_to(heads[None], (n_tp,) + heads.shape), "tp", 0, 0)

    columns = features // n_tp
    parts = out_weight.reshape(-1, n_tp, columns).swapaxes(0, 1)
    weight = lax.all_to_all(parts, "tp", 0, 0)
    piece = project_out(tp_at, gathered, weight, image, mod_gate.reshape(1, -1), out_bias.reshape(1, -1))
    pieces = lax.all_to_all(jnp.broadcast_to(piece[None], (n_tp,) + piece.shape), "tp", 0, 0)
    mixed = pieces.swapaxes(0, 1).reshape(rows, features)
    return (mixed, fresh_kv)


def solution(mesh):
    placed = (
        P("patch", None),
        P(),
        P(),
        P(),
        P(None, None, "tp"),
        P(None, "tp"),
        P(),
        P(),
        P(None, "patch", "tp"),
        P(None, None, "tp"),
        P("tp", None),
        P(),
    )
    return jax.shard_map(
        shards,
        mesh=mesh,
        in_specs=placed,
        out_specs=(P("patch", None), P(None, "patch", "tp")),
        check_vma=False,
    )
```

```python
import math

import jax
import jax.numpy as jnp
from jax import lax
from jax.experimental import pallas as pl
from jax.experimental.pallas import tpu as pltpu
from jax.sharding import PartitionSpec as P

BF = jnp.bfloat16
F32 = jnp.float32
VMEM = pl.BlockSpec(memory_space=pltpu.VMEM)
SMEM = pl.BlockSpec(memory_space=pltpu.SMEM)
LIMIT = 48 * 1024 * 1024


def params(**kw):
    return pltpu.CompilerParams(vmem_limit_bytes=LIMIT, **kw)


def prepare_kernel(c_ref, image_ref, shift_ref, scale_ref, stale_ref, mod_ref, mine_ref, theirs_ref):
    hd = mine_ref.shape[2]
    core = c_ref[0]
    mine_ref[...] = stale_ref[:, :, pl.ds(pl.multiple_of(core * hd, hd), hd)]
    theirs_ref[...] = stale_ref[:, :, pl.ds(pl.multiple_of((1 - core) * hd, hd), hd)]
    step = 32
    for i in range(image_ref.shape[0] // step):
        at = slice(i * step, (i + 1) * step)
        wide = image_ref[at, :].astype(F32)
        average = jnp.mean(wide, -1, keepdims=True)
        centred = wide - average
        spread = jnp.mean(centred * centred, -1, keepdims=True)
        normed = centred * lax.rsqrt(spread + 1e-06)
        mod_ref[at, :] = (normed * (1.0 + scale_ref[...]) + shift_ref[...]).astype(BF)


def prepare(core, image, shift, scale, stale, hd):
    return pl.pallas_call(
        prepare_kernel,
        in_specs=[SMEM] + [VMEM] * 4,
        out_specs=[VMEM] * 3,
        out_shape=[
            jax.ShapeDtypeStruct(image.shape, BF),
            jax.ShapeDtypeStruct(stale.shape[:2] + (hd,), BF),
            jax.ShapeDtypeStruct(stale.shape[:2] + (hd,), BF),
        ],
        compiler_params=params(),
        name="prepare",
    )(core, image, shift, scale, stale)


def project_kernel(c_ref, own_ref, other_ref, w_ref, bias_ref, q_gain_ref, k_gain_ref, q_ref, kv_own_ref, kv_other_ref, acc_ref):
    k = pl.program_id(0)
    rows = own_ref.shape[0]
    hd = q_gain_ref.shape[1]
    w = w_ref[...].reshape(3 * hd, w_ref.shape[2])

    @pl.when(k == 0)
    def _():
        acc_ref[...] = jnp.zeros_like(acc_ref)

    for i, m_ref in enumerate((own_ref, other_ref)):
        acc_ref[pl.ds(i * rows, rows), :] += lax.dot_general(
            m_ref[...], w, (((1,), (1,)), ((), ())), preferred_element_type=F32
        )

    def norm(part, gain):
        return part * lax.rsqrt(jnp.mean(part * part, -1, keepdims=True) + 1e-06) * gain

    @pl.when(k == pl.num_programs(0) - 1)
    def _():
        q = acc_ref[:, :hd] + bias_ref[0:1, :]
        q_ref[...] = norm(q, q_gain_ref[...]).astype(BF)
        for i, out_ref in enumerate((kv_own_ref, kv_other_ref)):
            at = pl.ds(i * rows, rows)
            out_ref[0] = norm(acc_ref[at, hd : 2 * hd] + bias_ref[1:2, :], k_gain_ref[...]).astype(BF)
            out_ref[1] = (acc_ref[at, 2 * hd :] + bias_ref[2:3, :]).astype(BF)


def project(core, own, other, weight, bias, q_gain, k_gain):
    rows, features = own.shape
    hd = q_gain.shape[1]
    depth = features // 4
    whole = lambda shape: pl.BlockSpec(shape, lambda k, c: (0,) * len(shape))
    return pl.pallas_call(
        project_kernel,
        grid_spec=pltpu.PrefetchScalarGridSpec(
            num_scalar_prefetch=1,
            grid=(features // depth,),
            in_specs=[
                pl.BlockSpec((rows, depth), lambda k, c: (0, k)),
                pl.BlockSpec((rows, depth), lambda k, c: (0, k)),
                pl.BlockSpec((3, hd, depth), lambda k, c: (0, c[0], k)),
                pl.BlockSpec((3, hd), lambda k, c: (0, c[0])),
                whole((1, hd)),
                whole((1, hd)),
            ],
            out_specs=[whole((2 * rows, hd)), whole((2, rows, hd)), whole((2, rows, hd))],
            scratch_shapes=[pltpu.VMEM((2 * rows, 3 * hd), F32)],
        ),
        out_shape=[
            jax.ShapeDtypeStruct((2 * rows, hd), BF),
            jax.ShapeDtypeStruct((2, rows, hd), BF),
            jax.ShapeDtypeStruct((2, rows, hd), BF),
        ],
        compiler_params=params(),
        name="project",
    )(core, own, other, weight, bias, q_gain, k_gain)


def block_sums(q, k, v_ref_value):
    hd = q.shape[1]
    scores = lax.dot_general(q, k, (((1,), (1,)), ((), ())), preferred_element_type=F32)
    weights = jnp.exp2(scores * (math.log2(math.e) / math.sqrt(hd))).astype(BF)
    ones = jnp.ones_like(v_ref_value)
    return jnp.dot(weights, jnp.concatenate([v_ref_value, ones], 1), preferred_element_type=F32)


def eye(n):
    return (lax.broadcasted_iota(jnp.int32, (n, n), 0) == lax.broadcasted_iota(jnp.int32, (n, n), 1)).astype(F32)


def remote_kernel(q_ref, kv_ref, out_ref):
    rows, hd = q_ref.shape
    same = eye(hd)
    for i in range(rows // hd):
        at = slice(i * hd, (i + 1) * hd)
        q = q_ref[at, :]
        total = None
        for j in range(kv_ref.shape[0]):
            part = block_sums(q, kv_ref[j, 0], kv_ref[j, 1])
            total = part if total is None else total + part
        out_ref[at, :] = total[:, :hd].astype(BF)
        line = jnp.sum(total[:, hd:] * same, 0, keepdims=True)
        high = line.astype(BF).astype(F32)
        out_ref[pl.ds(rows + 16 * i, 16), :] = jnp.concatenate(
            [jnp.broadcast_to(high, (8, hd)), jnp.broadcast_to(line - high, (8, hd))], 0
        ).astype(BF)


def attend_remote(q, kv):
    rows, hd = q.shape
    return pl.pallas_call(
        remote_kernel,
        in_specs=[VMEM] * 2,
        out_specs=VMEM,
        out_shape=jax.ShapeDtypeStruct((rows + 16 * (rows // hd), hd), BF),
        compiler_params=params(),
        name="attend_remote",
    )(q, kv)


def local_kernel(c_ref, q_ref, own_ref, other_ref, kv_ref, text_ref, out_ref):
    rows = own_ref.shape[1]
    hd = q_ref.shape[1]
    n = kv_ref.shape[0]
    slot = c_ref[1]
    head = pl.ds(pl.multiple_of(c_ref[0] * hd, hd), hd)
    for i, fresh in enumerate((own_ref, other_ref)):
        at = pl.ds(i * rows, rows)
        q = q_ref[at, :]
        stale = pl.ds((1 - i) * rows, rows)
        total = block_sums(q, fresh[0], fresh[1])
        total += block_sums(q, kv_ref[slot, 0, stale, :], kv_ref[slot, 1, stale, :])
        total += block_sums(q, text_ref[0, :, head], text_ref[1, :, head])
        for j in range(1, n):
            there = lax.rem(slot + j, n)
            total += block_sums(q, kv_ref[there, 0], kv_ref[there, 1])
        out_ref[at, :] = total


def attend_local(core_slot, q, own, other, kv, text):
    rows, hd = q.shape
    return pl.pallas_call(
        local_kernel,
        in_specs=[SMEM] + [VMEM] * 5,
        out_specs=VMEM,
        out_shape=jax.ShapeDtypeStruct((rows, 2 * hd), F32),
        compiler_params=params(),
        name="attend_local",
    )(core_slot, q, own, other, kv, text)


def combine_kernel(local_ref, p1_ref, p2_ref, p3_ref, own_ref, other_ref):
    rows, hd = local_ref.shape[0], own_ref.shape[1]
    same = eye(hd)
    for i in range(rows // hd):
        at = slice(i * hd, (i + 1) * hd)
        summed = local_ref[at, :hd]
        totals = local_ref[at, hd:]
        line = None
        for p in (p1_ref, p2_ref, p3_ref):
            summed += p[at, :].astype(F32)
            pair = p[pl.ds(rows + 16 * i, 16), :].astype(F32)
            both = pair[0:1] + pair[8:9]
            line = both if line is None else line + both
        column = jnp.sum(jnp.broadcast_to(line, (hd, hd)) * same, 1, keepdims=True)
        done = (summed / (totals + column)).astype(BF)
        half = rows // 2
        for out_ref, start in ((own_ref, 0), (other_ref, half)):
            low, high = max(i * hd, start), min((i + 1) * hd, start + half)
            if low < high:
                out_ref[low - start : high - start, :] = done[low - i * hd : high - i * hd]


def combine(local, parts):
    rows, hd = local.shape[0], local.shape[1] // 2
    return pl.pallas_call(
        combine_kernel,
        in_specs=[VMEM] * 4,
        out_specs=[VMEM] * 2,
        out_shape=[jax.ShapeDtypeStruct((rows // 2, hd), BF)] * 2,
        compiler_params=params(),
        name="combine",
    )(local, *parts)


def spread_kernel(c_ref, kept_ref, swapped_ref, out_ref):
    n, rows, width = out_ref.shape
    hd = width // 2
    core = c_ref[0]
    mine = pl.ds(pl.multiple_of(core * hd, hd), hd)
    theirs = pl.ds(pl.multiple_of((1 - core) * hd, hd), hd)
    for i in range(n):
        out_ref[i, :, mine] = kept_ref[...]
        out_ref[i, :, theirs] = swapped_ref[...]


def spread(core, kept, swapped, n):
    rows, hd = kept.shape
    return pl.pallas_call(
        spread_kernel,
        in_specs=[SMEM, VMEM, VMEM],
        out_specs=VMEM,
        out_shape=jax.ShapeDtypeStruct((n, rows, 2 * hd), BF),
        compiler_params=params(),
        name="spread",
    )(core, kept, swapped)


def cut_kernel(x_ref, out_ref):
    out_ref[0] = x_ref[...]


def cut(x, n):
    rows, features = x.shape
    columns = features // n
    return pl.pallas_call(
        cut_kernel,
        grid=(n,),
        in_specs=[pl.BlockSpec((rows, columns), lambda i: (0, i))],
        out_specs=pl.BlockSpec((1, rows, columns), lambda i: (i, 0, 0)),
        out_shape=jax.ShapeDtypeStruct((n, rows, columns), BF),
        compiler_params=params(),
        name="cut",
    )(x)


def out_kernel(t_ref, a_ref, w_ref, image_ref, gate_ref, bias_ref, out_ref):
    n = a_ref.shape[0]
    acc = None
    for i in range(n):
        part = jnp.dot(a_ref[i], w_ref[i], preferred_element_type=F32)
        acc = part if acc is None else acc + part
    projection = acc + bias_ref[...]
    piece = (image_ref[...].astype(F32) + gate_ref[...] * projection).astype(BF)
    for i in range(n):
        out_ref[i] = piece


def project_out(tp, gathered, weight, image, gate, bias):
    n, rows, width = gathered.shape
    columns = weight.shape[2]
    return pl.pallas_call(
        out_kernel,
        grid_spec=pltpu.PrefetchScalarGridSpec(
            num_scalar_prefetch=1,
            grid=(1,),
            in_specs=[
                pl.BlockSpec((n, rows, width), lambda k, t: (0, 0, 0)),
                pl.BlockSpec((n, width, columns), lambda k, t: (0, 0, 0)),
                pl.BlockSpec((rows, columns), lambda k, t: (0, t[0])),
                pl.BlockSpec((1, columns), lambda k, t: (0, t[0])),
                pl.BlockSpec((1, columns), lambda k, t: (0, t[0])),
            ],
            out_specs=pl.BlockSpec((n, rows, columns), lambda k, t: (0, 0, 0)),
        ),
        out_shape=jax.ShapeDtypeStruct((n, rows, columns), BF),
        compiler_params=params(),
        name="project_out",
    )(tp, gathered, weight, image, gate, bias)


def shards(image, mod_shift, mod_scale, mod_gate, qkv_weight, qkv_bias, q_gain, k_gain, stale_kv, text_kv, out_weight, out_bias):
    hd = q_gain.shape[0]
    rows, features = image.shape
    n_patch = lax.axis_size("patch")
    n_tp = lax.axis_size("tp")
    patch = lax.axis_index("patch")
    tp = lax.axis_index("tp")
    core = patch % 2
    slot = (patch // 4) % 4
    core_at = jnp.stack([core, slot]).astype(jnp.int32)
    tp_at = tp.astype(jnp.int32).reshape(1)

    def flip(bits):
        return [(i, i ^ bits) for i in range(n_patch)]

    def send(x, perm):
        return lax.ppermute(x, "patch", perm)

    groups = [[(i & ~12) | (4 * j) for j in range(4)] for i in range(n_patch) if not i & 12]

    shift = mod_shift.reshape(1, -1)
    scale = mod_scale.reshape(1, -1)
    modulated, mine, theirs = prepare(core_at, image, shift, scale, stale_kv, hd)
    kv_chip = jnp.concatenate([mine, send(theirs, flip(1))], 1)
    kv = lax.all_gather(kv_chip, "patch", axis_index_groups=groups)

    other = send(modulated, flip(1))
    gains = (q_gain.reshape(1, -1), k_gain.reshape(1, -1))
    wide = jnp.transpose(qkv_weight, (1, 2, 0))
    q, kv_own, kv_other = project(core_at, modulated, other, wide, qkv_bias, *gains)

    hops = (2, 16, 18)
    partial = []
    for bits in hops:
        there = send(q, flip(bits))
        partial.append(send(attend_remote(there, kv), flip(bits)))
    local = attend_local(core_at, q, kv_own, kv_other, kv, text_kv)
    kept, leaving = combine(local, partial)

    back = send(kv_other, flip(1))
    first = core == 0
    fresh_kv = jnp.where(first, jnp.concatenate([kv_own, back], 2), jnp.concatenate([back, kv_own], 2))

    heads = spread(core_at, kept, send(leaving, flip(1)), n_tp)
    gathered = lax.all_to_all(heads, "tp", 0, 0)

    late_weight, _ = lax.optimization_barrier((out_weight, q))
    weight = lax.all_to_all(cut(late_weight, n_tp), "tp", 0, 0)
    pieces = project_out(tp_at, gathered, weight, image, mod_gate.reshape(1, -1), out_bias.reshape(1, -1))
    pieces = lax.all_to_all(pieces, "tp", 0, 0)
    mixed = pieces.swapaxes(0, 1).reshape(rows, features)
    return (mixed, fresh_kv)


def solution(mesh):
    placed = (
        P("patch", None),
        P(),
        P(),
        P(),
        P(None, None, "tp"),
        P(None, "tp"),
        P(),
        P(),
        P(None, "patch", "tp"),
        P(None, None, "tp"),
        P("tp", None),
        P(),
    )
    return jax.shard_map(
        shards,
        mesh=mesh,
        in_specs=placed,
        out_specs=(P("patch", None), P(None, "patch", "tp")),
        check_vma=False,
    )
```

```python
import math

import jax
import jax.numpy as jnp
from jax import lax
from jax.experimental import pallas as pl
from jax.experimental.pallas import tpu as pltpu
from jax.sharding import PartitionSpec as P

BF = jnp.bfloat16
F32 = jnp.float32
VMEM = pl.BlockSpec(memory_space=pltpu.VMEM)
SMEM = pl.BlockSpec(memory_space=pltpu.SMEM)
HBM = pl.BlockSpec(memory_space=pltpu.HBM)
ANY = pl.BlockSpec(memory_space=pl.ANY)
LIMIT = 48 * 1024 * 1024


def params(**kw):
    return pltpu.CompilerParams(vmem_limit_bytes=LIMIT, **kw)


def fetch(pairs, sems):
    copies = [pltpu.make_async_copy(src, dst, sems.at[i]) for i, (src, dst) in enumerate(pairs)]
    for copy in copies:
        copy.start()
    return copies


def copies_kernel(stale_ref, out_ref, sems):
    n, _, _, hd = out_ref.shape
    heads = stale_ref.shape[2] // hd
    copies = fetch([(stale_ref.at[:, :, pl.ds(i % heads * hd, hd)], out_ref.at[i]) for i in range(n)], sems)
    for copy in copies:
        copy.wait()


def copies_of(stale, n, hd):
    return pl.pallas_call(
        copies_kernel,
        in_specs=[HBM],
        out_specs=HBM,
        out_shape=jax.ShapeDtypeStruct((n,) + stale.shape[:2] + (hd,), BF),
        scratch_shapes=[pltpu.SemaphoreType.DMA((n,))],
        compiler_params=params(),
        name="copies_of",
    )(stale)


def modulate_kernel(image_ref, shift_ref, scale_ref, mod_ref, image, shift, scale, sems):
    copies = fetch([(shift_ref, shift), (scale_ref, scale)], sems)
    rows = image_ref.shape[0]
    parts = 4
    part = rows // parts
    blocks = [
        pltpu.make_async_copy(image_ref.at[pl.ds(j * part, part)], image.at[pl.ds(j * part, part)], sems.at[2 + j])
        for j in range(parts)
    ]
    for copy in blocks:
        copy.start()
    for copy in copies:
        copy.wait()
    step = 16
    for j in range(parts):
        blocks[j].wait()
        for i in range(j * part // step, (j + 1) * part // step):
            at = slice(i * step, (i + 1) * step)
            wide = image[at, :].astype(F32)
            average = jnp.mean(wide, -1, keepdims=True)
            centred = wide - average
            spread = jnp.mean(centred * centred, -1, keepdims=True)
            normed = centred * lax.rsqrt(spread + 1e-06)
            mod_ref[at, :] = (normed * (1.0 + scale[...]) + shift[...]).astype(BF)


def modulate(image, shift, scale):
    return pl.pallas_call(
        modulate_kernel,
        in_specs=[HBM] * 3,
        out_specs=VMEM,
        out_shape=jax.ShapeDtypeStruct(image.shape, BF),
        scratch_shapes=[
            pltpu.VMEM(image.shape, BF),
            pltpu.VMEM(shift.shape, F32),
            pltpu.VMEM(scale.shape, F32),
            pltpu.SemaphoreType.DMA((6,)),
        ],
        compiler_params=params(),
        name="modulate",
    )(image, shift, scale)


def project_kernel(c_ref, own_ref, other_ref, w_ref, bias_ref, q_gain_ref, k_gain_ref, q_ref, kv_own_ref, kv_other_ref, wide, sems):
    rows, features = own_ref.shape
    hd = q_gain_ref.shape[1]
    home = pl.ds(pl.multiple_of(c_ref[0] * hd, hd), hd)
    parts = 4
    depth = features // parts
    copies = []
    for k in range(parts):
        at = pl.ds(k * depth, depth)
        copies += fetch(
            [(w_ref.at[j, at, home], wide.at[at, pl.ds(j * hd, hd)]) for j in range(3)], sems.at[pl.ds(3 * k, 3)]
        )
    sums = [None, None]
    for k in range(parts):
        for copy in copies[3 * k : 3 * k + 3]:
            copy.wait()
        at = slice(k * depth, (k + 1) * depth)
        for i, m_ref in enumerate((own_ref, other_ref)):
            term = jnp.dot(m_ref[:, at], wide[at, :], preferred_element_type=F32)
            sums[i] = term if k == 0 else sums[i] + term

    def norm(part, gain):
        return part * lax.rsqrt(jnp.mean(part * part, -1, keepdims=True) + 1e-06) * gain

    for i, out_ref in enumerate((kv_own_ref, kv_other_ref)):
        q = sums[i][:, :hd] + bias_ref[0:1, home]
        q_ref[pl.ds(i * rows, rows), :] = norm(q, q_gain_ref[...]).astype(BF)
        out_ref[0] = norm(sums[i][:, hd : 2 * hd] + bias_ref[1:2, home], k_gain_ref[...]).astype(BF)
        out_ref[1] = (sums[i][:, 2 * hd :] + bias_ref[2:3, home]).astype(BF)


def project(core, own, other, weight, bias, q_gain, k_gain):
    rows, features = own.shape
    hd = q_gain.shape[1]
    return pl.pallas_call(
        project_kernel,
        in_specs=[SMEM, VMEM, VMEM, ANY, VMEM, VMEM, VMEM],
        out_specs=[VMEM] * 3,
        out_shape=[
            jax.ShapeDtypeStruct((2 * rows, hd), BF),
            jax.ShapeDtypeStruct((2, rows, hd), BF),
            jax.ShapeDtypeStruct((2, rows, hd), BF),
        ],
        scratch_shapes=[pltpu.VMEM((features, 3 * hd), BF), pltpu.SemaphoreType.DMA((12,))],
        compiler_params=params(),
        name="project",
    )(core, own, other, jnp.transpose(weight, (1, 0, 2)), bias, q_gain, k_gain)


def block_sums(q, k, v_ref_value):
    hd = q.shape[1]
    scores = lax.dot_general(q, k, (((1,), (1,)), ((), ())), preferred_element_type=F32)
    weights = jnp.exp2(scores * (math.log2(math.e) / math.sqrt(hd))).astype(BF)
    ones = jnp.ones_like(v_ref_value)
    return jnp.dot(weights, jnp.concatenate([v_ref_value, ones], 1), preferred_element_type=F32)


def eye(n):
    return (lax.broadcasted_iota(jnp.int32, (n, n), 0) == lax.broadcasted_iota(jnp.int32, (n, n), 1)).astype(F32)


def remote_kernel(q_ref, kv_ref, out_ref):
    rows, hd = q_ref.shape
    same = eye(hd)
    for i in range(rows // hd):
        at = slice(i * hd, (i + 1) * hd)
        q = q_ref[at, :]
        total = None
        for j in range(0, kv_ref.shape[0], 2):
            k, v = (kv_ref[j : j + 2, part].reshape(-1, hd) for part in (0, 1))
            part = block_sums(q, k, v)
            total = part if total is None else total + part
        out_ref[at, :] = total[:, :hd].astype(BF)
        line = jnp.sum(total[:, hd:] * same, 0, keepdims=True)
        high = line.astype(BF).astype(F32)
        out_ref[pl.ds(rows + 16 * i, 16), :] = jnp.concatenate(
            [jnp.broadcast_to(high, (8, hd)), jnp.broadcast_to(line - high, (8, hd))], 0
        ).astype(BF)


def attend_remote(q, kv):
    rows, hd = q.shape
    return pl.pallas_call(
        remote_kernel,
        in_specs=[VMEM] * 2,
        out_specs=VMEM,
        out_shape=jax.ShapeDtypeStruct((rows + 16 * (rows // hd), hd), BF),
        compiler_params=params(),
        name="attend_remote",
    )(q, kv)


def local_kernel(c_ref, q_ref, own_ref, other_ref, kv_ref, text_ref, out_ref):
    rows = own_ref.shape[1]
    hd = q_ref.shape[1]
    n = kv_ref.shape[0]
    core, chip = c_ref[0], c_ref[1]
    head = pl.ds(pl.multiple_of(core * hd, hd), hd)
    for i, fresh in enumerate((own_ref, other_ref)):
        at = pl.ds(i * rows, rows)
        q = q_ref[at, :]
        beside = 2 * chip + (1 - core if i == 0 else core)
        total = block_sums(q, fresh[0], fresh[1])
        total += block_sums(q, kv_ref[beside, 0], kv_ref[beside, 1])
        total += block_sums(q, text_ref[0, :, head], text_ref[1, :, head])
        for j in range(1, n // 2):
            there = pl.ds(2 * lax.rem(chip + j, n // 2), 2)
            k, v = (kv_ref[there, part].reshape(-1, hd) for part in (0, 1))
            total += block_sums(q, k, v)
        out_ref[at, :] = total


def attend_local(core_slot, q, own, other, kv, text):
    rows, hd = q.shape
    return pl.pallas_call(
        local_kernel,
        in_specs=[SMEM] + [VMEM] * 5,
        out_specs=VMEM,
        out_shape=jax.ShapeDtypeStruct((rows, 2 * hd), F32),
        compiler_params=params(),
        name="attend_local",
    )(core_slot, q, own, other, kv, text)


def combine_kernel(local_ref, p1_ref, p2_ref, p3_ref, own_ref, other_ref):
    rows, hd = local_ref.shape[0], own_ref.shape[1]
    same = eye(hd)
    for i in range(rows // hd):
        at = slice(i * hd, (i + 1) * hd)
        summed = local_ref[at, :hd]
        totals = local_ref[at, hd:]
        line = None
        for p in (p1_ref, p2_ref, p3_ref):
            summed += p[at, :].astype(F32)
            pair = p[pl.ds(rows + 16 * i, 16), :].astype(F32)
            both = pair[0:1] + pair[8:9]
            line = both if line is None else line + both
        column = jnp.sum(jnp.broadcast_to(line, (hd, hd)) * same, 1, keepdims=True)
        done = (summed / (totals + column)).astype(BF)
        half = rows // 2
        for out_ref, start in ((own_ref, 0), (other_ref, half)):
            low, high = max(i * hd, start), min((i + 1) * hd, start + half)
            if low < high:
                out_ref[low - start : high - start, :] = done[low - i * hd : high - i * hd]


def combine(local, parts):
    rows, hd = local.shape[0], local.shape[1] // 2
    return pl.pallas_call(
        combine_kernel,
        in_specs=[VMEM] * 4,
        out_specs=[VMEM] * 2,
        out_shape=[jax.ShapeDtypeStruct((rows // 2, hd), BF)] * 2,
        compiler_params=params(),
        name="combine",
    )(local, *parts)


def terms_kernel(c_ref, kept_ref, swapped_ref, w_ref, out_ref, heads, pieces, sems):
    n, rows, columns = out_ref.shape
    hd = kept_ref.shape[1]
    core = c_ref[0]
    heads[:, pl.ds(pl.multiple_of(core * hd, hd), hd)] = kept_ref[...]
    heads[:, pl.ds(pl.multiple_of((1 - core) * hd, hd), hd)] = swapped_ref[...]
    copies = []
    for i in range(n):
        pieces[i] = jnp.dot(heads[...], w_ref[:, i * columns : (i + 1) * columns], preferred_element_type=F32).astype(BF)
        copies += fetch([(pieces.at[i], out_ref.at[i])], sems.at[pl.ds(i, 1)])
    for copy in copies:
        copy.wait()


def terms_of(core, kept, swapped, weight, n):
    rows, hd = kept.shape
    shape = (n, rows, weight.shape[1] // n)
    return pl.pallas_call(
        terms_kernel,
        in_specs=[SMEM, VMEM, VMEM, VMEM],
        out_specs=HBM,
        out_shape=jax.ShapeDtypeStruct(shape, BF),
        scratch_shapes=[pltpu.VMEM((rows, weight.shape[0]), BF), pltpu.VMEM(shape, BF), pltpu.SemaphoreType.DMA((n,))],
        compiler_params=params(),
        name="terms_of",
    )(core, kept, swapped, weight)


def mix_kernel(t_ref, terms_ref, image_ref, gate_ref, bias_ref, out_ref, piece, sems):
    n = terms_ref.shape[0]
    projection = terms_ref[0].astype(F32)
    for i in range(1, n):
        projection += terms_ref[i].astype(F32)
    projection += bias_ref[...]
    piece[...] = (image_ref[...].astype(F32) + gate_ref[...] * projection).astype(BF)
    for copy in fetch([(piece, out_ref.at[i]) for i in range(n)], sems):
        copy.wait()


def mix(tp, terms, image, gate, bias):
    n, rows, columns = terms.shape
    return pl.pallas_call(
        mix_kernel,
        grid_spec=pltpu.PrefetchScalarGridSpec(
            num_scalar_prefetch=1,
            grid=(1,),
            in_specs=[
                pl.BlockSpec((n, rows, columns), lambda k, t: (0, 0, 0)),
                pl.BlockSpec((rows, columns), lambda k, t: (0, t[0])),
                pl.BlockSpec((1, columns), lambda k, t: (0, t[0])),
                pl.BlockSpec((1, columns), lambda k, t: (0, t[0])),
            ],
            out_specs=HBM,
            scratch_shapes=[pltpu.VMEM((rows, columns), BF), pltpu.SemaphoreType.DMA((n,))],
        ),
        out_shape=jax.ShapeDtypeStruct((n, rows, columns), BF),
        compiler_params=params(),
        name="mix",
    )(tp, terms, image, gate, bias)


def join_kernel(pieces_ref, out_ref, sems):
    n, _, columns = pieces_ref.shape
    copies = fetch([(pieces_ref.at[i], out_ref.at[:, pl.ds(i * columns, columns)]) for i in range(n)], sems)
    for copy in copies:
        copy.wait()


def join(pieces):
    n, rows, columns = pieces.shape
    return pl.pallas_call(
        join_kernel,
        in_specs=[ANY],
        out_specs=HBM,
        out_shape=jax.ShapeDtypeStruct((rows, n * columns), BF),
        scratch_shapes=[pltpu.SemaphoreType.DMA((n,))],
        compiler_params=params(),
        name="join",
    )(pieces)


def shards(image, mod_shift, mod_scale, mod_gate, qkv_weight, qkv_bias, q_gain, k_gain, stale_kv, text_kv, out_weight, out_bias):
    hd = q_gain.shape[0]
    rows, features = image.shape
    n_patch = lax.axis_size("patch")
    n_tp = lax.axis_size("tp")
    patch = lax.axis_index("patch")
    tp = lax.axis_index("tp")
    core = patch % 2
    slot = (patch // 4) % 4
    core_at = jnp.stack([core, slot]).astype(jnp.int32)
    tp_at = tp.astype(jnp.int32).reshape(1)

    def flip(bits):
        return [(i, i ^ bits) for i in range(n_patch)]

    def send(x, perm):
        return lax.ppermute(x, "patch", perm)

    groups = [[i | 4 * j | c for j in range(4) for c in (0, 1)] for i in range(n_patch) if not i & 13]

    modulated = modulate(image, mod_shift.reshape(1, -1), mod_scale.reshape(1, -1))
    other = send(modulated, flip(1))
    copies = copies_of(stale_kv, len(groups[0]), hd)
    kv = lax.all_to_all(copies, "patch", 0, 0, axis_index_groups=groups)
    gains = (q_gain.reshape(1, -1), k_gain.reshape(1, -1))
    q, kv_own, kv_other = project(core_at, modulated, other, qkv_weight, qkv_bias, *gains)

    hops = (2, 16, 18)
    partial = []
    for bits in hops:
        there = send(q, flip(bits))
        partial.append(send(attend_remote(there, kv), flip(bits)))
    local = attend_local(core_at, q, kv_own, kv_other, kv, text_kv)
    kept, leaving = combine(local, partial)

    back = send(kv_other, flip(1))
    first = core == 0
    fresh_kv = jnp.where(first, jnp.concatenate([kv_own, back], 2), jnp.concatenate([back, kv_own], 2))

    terms = terms_of(core_at, kept, send(leaving, flip(1)), out_weight, n_tp)
    terms = lax.all_to_all(terms, "tp", 0, 0)
    pieces = mix(tp_at, terms, image, mod_gate.reshape(1, -1), out_bias.reshape(1, -1))
    mixed = join(lax.all_to_all(pieces, "tp", 0, 0))
    return (mixed, fresh_kv)


def solution(mesh):
    placed = (
        P("patch", None),
        P(),
        P(),
        P(),
        P(None, None, "tp"),
        P(None, "tp"),
        P(),
        P(),
        P(None, "patch", "tp"),
        P(None, None, "tp"),
        P("tp", None),
        P(),
    )
    return jax.shard_map(
        shards,
        mesh=mesh,
        in_specs=placed,
        out_specs=(P("patch", None), P(None, "patch", "tp")),
        check_vma=False,
    )
```

```python
import math

import jax
import jax.numpy as jnp
from jax import lax
from jax.experimental import pallas as pl
from jax.experimental.pallas import tpu as pltpu
from jax.sharding import PartitionSpec as P

BF = jnp.bfloat16
F32 = jnp.float32
VMEM = pl.BlockSpec(memory_space=pltpu.VMEM)
SMEM = pl.BlockSpec(memory_space=pltpu.SMEM)
HBM = pl.BlockSpec(memory_space=pltpu.HBM)
ANY = pl.BlockSpec(memory_space=pl.ANY)
LIMIT = 16 * 1024 * 1024


def params(**kw):
    return pltpu.CompilerParams(vmem_limit_bytes=LIMIT, **kw)


def in_hbm(x):
    return pltpu.with_memory_space_constraint(x, pltpu.HBM)


def fetch(pairs, sems):
    copies = [pltpu.make_async_copy(src, dst, sems.at[i]) for i, (src, dst) in enumerate(pairs)]
    for copy in copies:
        copy.start()
    return copies


def copies_kernel(stale_ref, out_ref, held, sems):
    n, _, _, hd = out_ref.shape
    heads = stale_ref.shape[2] // hd
    for copy in fetch([(stale_ref.at[:, :, pl.ds(i * hd, hd)], held.at[i]) for i in range(heads)], sems):
        copy.wait()
    copies = fetch([(held.at[i % heads], out_ref.at[i]) for i in range(n)], sems)
    for copy in copies:
        copy.wait()


def copies_of(stale, n, hd):
    return pl.pallas_call(
        copies_kernel,
        in_specs=[HBM],
        out_specs=HBM,
        out_shape=jax.ShapeDtypeStruct((n,) + stale.shape[:2] + (hd,), BF),
        scratch_shapes=[
            pltpu.VMEM((stale.shape[2] // hd,) + stale.shape[:2] + (hd,), BF),
            pltpu.SemaphoreType.DMA((n,)),
        ],
        compiler_params=params(),
        name="copies_of",
    )(in_hbm(stale))


def modulate_kernel(image_ref, shift_ref, scale_ref, _, mod_ref, image, shift, scale, sems):
    copies = fetch([(shift_ref, shift), (scale_ref, scale)], sems)
    rows = image_ref.shape[0]
    parts = 4
    part = rows // parts
    blocks = [
        pltpu.make_async_copy(image_ref.at[pl.ds(j * part, part)], image.at[pl.ds(j * part, part)], sems.at[2 + j])
        for j in range(parts)
    ]
    for copy in blocks:
        copy.start()
    for copy in copies:
        copy.wait()
    gain = 1.0 + scale[...].reshape(1, -1)
    lift = shift[...].reshape(1, -1)
    step = 16
    for j in range(parts):
        blocks[j].wait()
        for i in range(j * part // step, (j + 1) * part // step):
            at = slice(i * step, (i + 1) * step)
            wide = image[at, :].astype(F32)
            average = jnp.mean(wide, -1, keepdims=True)
            centred = wide - average
            spread = jnp.mean(centred * centred, -1, keepdims=True)
            normed = centred * lax.rsqrt(spread + 1e-06)
            mod_ref[at, :] = (normed * gain + lift).astype(BF)


def modulate(image, shift, scale, awaited):
    return pl.pallas_call(
        modulate_kernel,
        in_specs=[HBM] * 3 + [ANY],
        out_specs=VMEM,
        out_shape=jax.ShapeDtypeStruct(image.shape, BF),
        scratch_shapes=[
            pltpu.VMEM(image.shape, BF),
            pltpu.VMEM(shift.shape, F32),
            pltpu.VMEM(scale.shape, F32),
            pltpu.SemaphoreType.DMA((6,)),
        ],
        compiler_params=params(),
        name="modulate",
    )(*(in_hbm(x) for x in (image, shift, scale)), awaited)


def finish_kernel(c_ref, sums_ref, bias_ref, q_gain_ref, k_gain_ref, fresh_ref, home_ref, away_ref):
    _, rows, width = sums_ref.shape
    hd = q_gain_ref.shape[1]

    def norm(part, gain):
        return part * lax.rsqrt(jnp.mean(part * part, -1, keepdims=True) + 1e-06) * gain

    for h in range(width // hd):
        at = slice(h * hd, (h + 1) * hd)
        q = norm(sums_ref[0, :, at] + bias_ref[0:1, at], q_gain_ref[...]).astype(BF)
        k = norm(sums_ref[1, :, at] + bias_ref[1:2, at], k_gain_ref[...]).astype(BF)
        v = (sums_ref[2, :, at] + bias_ref[2:3, at]).astype(BF)
        fresh_ref[0, :, at] = k
        fresh_ref[1, :, at] = v

        def put(out_ref, q=q, k=k, v=v):
            for j, x in enumerate((q, k, v)):
                out_ref[j] = x

        pl.when(c_ref[0] == h)(lambda: put(home_ref))
        pl.when(c_ref[0] != h)(lambda: put(away_ref))


def project(core, modulated, weight, bias, q_gain, k_gain):
    rows, features = modulated.shape
    hd = q_gain.shape[1]
    sums = jnp.einsum("tf,jfc->jtc", modulated, jnp.transpose(weight, (1, 0, 2)), preferred_element_type=F32)
    part = jax.ShapeDtypeStruct((3, rows, hd), BF)
    return pl.pallas_call(
        finish_kernel,
        in_specs=[SMEM] + [VMEM] * 4,
        out_specs=[VMEM] * 3,
        out_shape=[jax.ShapeDtypeStruct((2, rows, weight.shape[2]), BF), part, part],
        compiler_params=params(),
        name="finish",
    )(core, sums, bias, q_gain, k_gain)


def block_sums(q, k, v_ref_value):
    hd = q.shape[1]
    scores = lax.dot_general(q, k, (((1,), (1,)), ((), ())), preferred_element_type=F32)
    weights = jnp.exp2(scores * (math.log2(math.e) / math.sqrt(hd))).astype(BF)
    ones = jnp.ones_like(v_ref_value)
    return jnp.dot(weights, jnp.concatenate([v_ref_value, ones], 1), preferred_element_type=F32)


def eye(n):
    return (lax.broadcasted_iota(jnp.int32, (n, n), 0) == lax.broadcasted_iota(jnp.int32, (n, n), 1)).astype(F32)


def remote_kernel(q_ref, kv_ref, out_ref):
    rows, hd = q_ref.shape
    same = eye(hd)
    k, v = (kv_ref[:, part].reshape(-1, hd) for part in (0, 1))
    total = block_sums(q_ref[...], k, v)
    out_ref[pl.ds(0, rows), :] = total[:, :hd].astype(BF)
    for i in range(rows // hd):
        line = jnp.sum(total[i * hd : (i + 1) * hd, hd:] * same, 0, keepdims=True)
        high = line.astype(BF).astype(F32)
        out_ref[pl.ds(rows + 16 * i, 16), :] = jnp.concatenate(
            [jnp.broadcast_to(high, (8, hd)), jnp.broadcast_to(line - high, (8, hd))], 0
        ).astype(BF)


def attend_remote(q, kv):
    rows, hd = q.shape
    return pl.pallas_call(
        remote_kernel,
        in_specs=[VMEM] * 2,
        out_specs=VMEM,
        out_shape=jax.ShapeDtypeStruct((rows + 16 * (rows // hd), hd), BF),
        compiler_params=params(),
        name="attend_remote",
    )(q, kv)


def local_kernel(c_ref, q_ref, own_ref, other_ref, kv_ref, text_ref, out_ref):
    rows, hd = own_ref.shape[1:]
    head = pl.ds(pl.multiple_of(c_ref[0] * hd, hd), hd)
    core, chip, chips = c_ref[0], c_ref[1], kv_ref.shape[0] // 2
    out_ref[...] = block_sums(q_ref[...], text_ref[0, :, head], text_ref[1, :, head])
    for j in range(1, chips):
        there = pl.ds(2 * lax.rem(chip + j, chips), 2)
        k, v = (kv_ref[there, part].reshape(-1, hd) for part in (0, 1))
        out_ref[...] += block_sums(q_ref[...], k, v)
    for i, fresh in enumerate((own_ref.at[1:3], other_ref.at[1:3])):
        at = pl.ds(i * rows, rows)
        beside = 2 * chip + (1 - core if i == 0 else core)
        k, v = (jnp.concatenate([fresh[j], kv_ref[beside, j]], 0) for j in (0, 1))
        out_ref[at, :] += block_sums(q_ref[at, :], k, v)


def attend_local(core, q, own, other, kv, text):
    rows, hd = q.shape
    return pl.pallas_call(
        local_kernel,
        in_specs=[SMEM] + [VMEM] * 5,
        out_specs=VMEM,
        out_shape=jax.ShapeDtypeStruct((rows, 2 * hd), F32),
        compiler_params=params(),
        name="attend_local",
    )(core, q, own, other, kv, text)


def combine_kernel(local_ref, p1_ref, p2_ref, p3_ref, own_ref, other_ref):
    rows, hd = local_ref.shape[0], own_ref.shape[1]
    same = eye(hd)
    for i in range(rows // hd):
        at = slice(i * hd, (i + 1) * hd)
        summed = local_ref[at, :hd]
        totals = local_ref[at, hd:]
        line = None
        for p in (p1_ref, p2_ref, p3_ref):
            summed += p[at, :].astype(F32)
            pair = p[pl.ds(rows + 16 * i, 16), :].astype(F32)
            both = pair[0:1] + pair[8:9]
            line = both if line is None else line + both
        column = jnp.sum(jnp.broadcast_to(line, (hd, hd)) * same, 1, keepdims=True)
        done = (summed / (totals + column)).astype(BF)
        half = rows // 2
        for out_ref, start in ((own_ref, 0), (other_ref, half)):
            low, high = max(i * hd, start), min((i + 1) * hd, start + half)
            if low < high:
                out_ref[low - start : high - start, :] = done[low - i * hd : high - i * hd]


def combine(local, parts):
    rows, hd = local.shape[0], local.shape[1] // 2
    return pl.pallas_call(
        combine_kernel,
        in_specs=[VMEM] * 4,
        out_specs=[VMEM] * 2,
        out_shape=[jax.ShapeDtypeStruct((rows // 2, hd), BF)] * 2,
        compiler_params=params(),
        name="combine",
    )(local, *parts)


def terms_kernel(c_ref, kept_ref, swapped_ref, w_ref, out_ref, heads, pieces, sems):
    n, rows, columns = out_ref.shape
    hd = kept_ref.shape[1]
    core = c_ref[0]
    heads[:, pl.ds(pl.multiple_of(core * hd, hd), hd)] = kept_ref[...]
    heads[:, pl.ds(pl.multiple_of((1 - core) * hd, hd), hd)] = swapped_ref[...]
    copies = []
    for i in range(n):
        pieces[i] = jnp.dot(heads[...], w_ref[:, i * columns : (i + 1) * columns], preferred_element_type=F32).astype(BF)
        copies += fetch([(pieces.at[i], out_ref.at[i])], sems.at[pl.ds(i, 1)])
    for copy in copies:
        copy.wait()


def terms_of(core, kept, swapped, weight, n):
    rows, hd = kept.shape
    shape = (n, rows, weight.shape[1] // n)
    return pl.pallas_call(
        terms_kernel,
        in_specs=[SMEM, VMEM, VMEM, VMEM],
        out_specs=HBM,
        out_shape=jax.ShapeDtypeStruct(shape, BF),
        scratch_shapes=[pltpu.VMEM((rows, weight.shape[0]), BF), pltpu.VMEM(shape, BF), pltpu.SemaphoreType.DMA((n,))],
        compiler_params=params(),
        name="terms_of",
    )(core, kept, swapped, weight)


def mix_kernel(t_ref, terms_ref, image_ref, gate_ref, bias_ref, out_ref, piece, sems):
    n = terms_ref.shape[0]
    projection = terms_ref[0].astype(F32)
    for i in range(1, n):
        projection += terms_ref[i].astype(F32)
    projection += bias_ref[...]
    piece[...] = (image_ref[...].astype(F32) + gate_ref[...] * projection).astype(BF)
    for copy in fetch([(piece, out_ref.at[i]) for i in range(n)], sems):
        copy.wait()


def mix(tp, terms, image, gate, bias):
    n, rows, columns = terms.shape
    return pl.pallas_call(
        mix_kernel,
        grid_spec=pltpu.PrefetchScalarGridSpec(
            num_scalar_prefetch=1,
            grid=(1,),
            in_specs=[
                pl.BlockSpec((n, rows, columns), lambda k, t: (0, 0, 0)),
                pl.BlockSpec((rows, columns), lambda k, t: (0, t[0])),
                pl.BlockSpec((1, columns), lambda k, t: (0, t[0])),
                pl.BlockSpec((1, columns), lambda k, t: (0, t[0])),
            ],
            out_specs=HBM,
            scratch_shapes=[pltpu.VMEM((rows, columns), BF), pltpu.SemaphoreType.DMA((n,))],
        ),
        out_shape=jax.ShapeDtypeStruct((n, rows, columns), BF),
        compiler_params=params(),
        name="mix",
    )(tp, terms, image, gate, bias)


def join_kernel(pieces_ref, out_ref, sems):
    n, _, columns = pieces_ref.shape
    copies = fetch([(pieces_ref.at[i], out_ref.at[:, pl.ds(i * columns, columns)]) for i in range(n)], sems)
    for copy in copies:
        copy.wait()


def join(pieces):
    n, rows, columns = pieces.shape
    return pl.pallas_call(
        join_kernel,
        in_specs=[ANY],
        out_specs=HBM,
        out_shape=jax.ShapeDtypeStruct((rows, n * columns), BF),
        scratch_shapes=[pltpu.SemaphoreType.DMA((n,))],
        compiler_params=params(),
        name="join",
    )(pieces)


def shards(image, mod_shift, mod_scale, mod_gate, qkv_weight, qkv_bias, q_gain, k_gain, stale_kv, text_kv, out_weight, out_bias):
    hd = q_gain.shape[0]
    rows, features = image.shape
    n_patch = lax.axis_size("patch")
    n_tp = lax.axis_size("tp")
    patch = lax.axis_index("patch")
    tp = lax.axis_index("tp")
    core = patch % 2
    chip = (patch // 16) * 2 + (patch // 2) % 2
    core_at = jnp.stack([core, chip]).astype(jnp.int32)
    tp_at = tp.astype(jnp.int32).reshape(1)

    def flip(bits):
        return [(i, i ^ bits) for i in range(n_patch)]

    def turn(k):
        return [(i, (i & ~12) | ((i + 4 * k) & 12)) for i in range(n_patch)]

    def send(x, perm):
        return lax.ppermute(x, "patch", perm)

    groups = [[i | y | z | c for y in (0, 16) for z in (0, 2) for c in (0, 1)] for i in range(n_patch) if not i & 19]
    copies = copies_of(stale_kv, len(groups[0]), hd)
    kv = lax.all_to_all(copies, "patch", 0, 0, axis_index_groups=groups)

    modulated = modulate(image, mod_shift, mod_scale, copies)
    gains = (q_gain.reshape(1, -1), k_gain.reshape(1, -1))
    fresh_kv, own, away = project(core_at, modulated, qkv_weight, qkv_bias, *gains)
    other = send(away, flip(1))
    q = jnp.concatenate([own[0], other[0]], 0)

    partial = []
    for k in (1, 3, 2):
        there = send(q, turn(k))
        partial.append(send(attend_remote(there, kv), turn(4 - k)))
    local = attend_local(core_at, q, own, other, kv, text_kv)
    kept, leaving = combine(local, partial)

    terms = terms_of(core_at, kept, send(leaving, flip(1)), out_weight, n_tp)
    terms = lax.all_to_all(terms, "tp", 0, 0)
    pieces = mix(tp_at, terms, image, mod_gate.reshape(1, -1), out_bias.reshape(1, -1))
    mixed = join(lax.all_to_all(pieces, "tp", 0, 0))
    return (mixed, fresh_kv)


def solution(mesh):
    placed = (
        P("patch", None),
        P(),
        P(),
        P(),
        P(None, None, "tp"),
        P(None, "tp"),
        P(),
        P(),
        P(None, "patch", "tp"),
        P(None, None, "tp"),
        P("tp", None),
        P(),
    )
    return jax.shard_map(
        shards,
        mesh=mesh,
        in_specs=placed,
        out_specs=(P("patch", None), P(None, "patch", "tp")),
        check_vma=False,
    )
```

```python
import math

import jax
import jax.numpy as jnp
from jax import lax
from jax.experimental import pallas as pl
from jax.experimental.pallas import tpu as pltpu
from jax.sharding import PartitionSpec as P

BF = jnp.bfloat16
F32 = jnp.float32
VMEM = pl.BlockSpec(memory_space=pltpu.VMEM)
SMEM = pl.BlockSpec(memory_space=pltpu.SMEM)
HBM = pl.BlockSpec(memory_space=pltpu.HBM)
ANY = pl.BlockSpec(memory_space=pl.ANY)
LIMIT = 16 * 1024 * 1024


def params(**kw):
    return pltpu.CompilerParams(vmem_limit_bytes=LIMIT, **kw)


def in_hbm(x):
    return pltpu.with_memory_space_constraint(x, pltpu.HBM)


def fetch(pairs, sems):
    copies = [pltpu.make_async_copy(src, dst, sems.at[i]) for i, (src, dst) in enumerate(pairs)]
    for copy in copies:
        copy.start()
    return copies


def copies_kernel(stale_ref, out_ref, held, sems):
    n, _, _, hd = out_ref.shape
    heads = stale_ref.shape[2] // hd
    for copy in fetch([(stale_ref.at[:, :, pl.ds(i * hd, hd)], held.at[i]) for i in range(heads)], sems):
        copy.wait()
    copies = fetch([(held.at[i % heads], out_ref.at[i]) for i in range(n)], sems)
    for copy in copies:
        copy.wait()


def copies_of(stale, n, hd):
    return pl.pallas_call(
        copies_kernel,
        in_specs=[HBM],
        out_specs=HBM,
        out_shape=jax.ShapeDtypeStruct((n,) + stale.shape[:2] + (hd,), BF),
        scratch_shapes=[
            pltpu.VMEM((stale.shape[2] // hd,) + stale.shape[:2] + (hd,), BF),
            pltpu.SemaphoreType.DMA((n,)),
        ],
        compiler_params=params(),
        name="copies_of",
    )(in_hbm(stale))


def modulate_kernel(image_ref, shift_ref, scale_ref, w_ref, _, mod_ref, near_ref, image, shift, scale, sems):
    brought = pltpu.make_async_copy(w_ref, near_ref, sems.at[6])
    copies = fetch([(shift_ref, shift), (scale_ref, scale)], sems)
    rows = image_ref.shape[0]
    parts = 4
    part = rows // parts
    blocks = [
        pltpu.make_async_copy(image_ref.at[pl.ds(j * part, part)], image.at[pl.ds(j * part, part)], sems.at[2 + j])
        for j in range(parts)
    ]
    for copy in blocks:
        copy.start()
    brought.start()
    for copy in copies:
        copy.wait()
    gain = 1.0 + scale[...].reshape(1, -1)
    lift = shift[...].reshape(1, -1)
    step = 16
    for j in range(parts):
        blocks[j].wait()
        for i in range(j * part // step, (j + 1) * part // step):
            at = slice(i * step, (i + 1) * step)
            wide = image[at, :].astype(F32)
            average = jnp.mean(wide, -1, keepdims=True)
            centred = wide - average
            spread = jnp.mean(centred * centred, -1, keepdims=True)
            normed = centred * lax.rsqrt(spread + 1e-06)
            mod_ref[at, :] = (normed * gain + lift).astype(BF)
    brought.wait()


def modulate(image, shift, scale, weight, awaited):
    return pl.pallas_call(
        modulate_kernel,
        in_specs=[ANY] * 3 + [HBM, ANY],
        out_specs=[VMEM] * 2,
        out_shape=[jax.ShapeDtypeStruct(image.shape, BF), jax.ShapeDtypeStruct(weight.shape, BF)],
        scratch_shapes=[
            pltpu.VMEM(image.shape, BF),
            pltpu.VMEM(shift.shape, F32),
            pltpu.VMEM(scale.shape, F32),
            pltpu.SemaphoreType.DMA((7,)),
        ],
        compiler_params=params(),
        name="modulate",
    )(image, shift, scale, in_hbm(weight), awaited)


def finish_kernel(c_ref, sums_ref, bias_ref, q_gain_ref, k_gain_ref, fresh_ref, home_ref, away_ref):
    hd = q_gain_ref.shape[1]
    first = c_ref[0] == 0

    def norm(part, gain):
        return part * lax.rsqrt(jnp.mean(part * part, -1, keepdims=True) + 1e-06) * gain

    for j, gain_ref in enumerate((q_gain_ref, k_gain_ref, None)):
        pair = []
        for at in (slice(0, hd), slice(hd, 2 * hd)):
            part = sums_ref[j, :, at] + bias_ref[j : j + 1, at]
            pair.append((part if gain_ref is None else norm(part, gain_ref[...])).astype(BF))
            if j > 0:
                fresh_ref[j - 1, :, at] = pair[-1]
        home_ref[j] = jnp.where(first, pair[0], pair[1])
        away_ref[j] = jnp.where(first, pair[1], pair[0])


def project(core, modulated, weight, bias, q_gain, k_gain):
    rows, features = modulated.shape
    hd = q_gain.shape[1]
    sums = jnp.einsum("tf,jfc->jtc", modulated, weight, preferred_element_type=F32)
    part = jax.ShapeDtypeStruct((3, rows, hd), BF)
    return pl.pallas_call(
        finish_kernel,
        in_specs=[SMEM] + [VMEM] * 4,
        out_specs=[VMEM] * 3,
        out_shape=[jax.ShapeDtypeStruct((2, rows, weight.shape[2]), BF), part, part],
        compiler_params=params(),
        name="finish",
    )(core, sums, bias, q_gain, k_gain)


def block_sums(q, k, v_ref_value):
    hd = q.shape[1]
    scores = lax.dot_general(q, k, (((1,), (1,)), ((), ())), preferred_element_type=F32)
    weights = jnp.exp2(scores * (math.log2(math.e) / math.sqrt(hd))).astype(BF)
    ones = jnp.ones_like(v_ref_value)
    return jnp.dot(weights, jnp.concatenate([v_ref_value, ones], 1), preferred_element_type=F32)


def eye(n):
    return (lax.broadcasted_iota(jnp.int32, (n, n), 0) == lax.broadcasted_iota(jnp.int32, (n, n), 1)).astype(F32)


def remote_kernel(q_ref, kv_ref, out_ref):
    rows, hd = q_ref.shape
    same = eye(hd)
    k, v = (kv_ref[:, part].reshape(-1, hd) for part in (0, 1))
    total = block_sums(q_ref[...], k, v)
    out_ref[pl.ds(0, rows), :] = total[:, :hd].astype(BF)
    for i in range(rows // hd):
        line = jnp.sum(total[i * hd : (i + 1) * hd, hd:] * same, 0, keepdims=True)
        high = line.astype(BF).astype(F32)
        out_ref[pl.ds(rows + 16 * i, 16), :] = jnp.concatenate(
            [jnp.broadcast_to(high, (8, hd)), jnp.broadcast_to(line - high, (8, hd))], 0
        ).astype(BF)


def attend_remote(q, kv):
    rows, hd = q.shape
    return pl.pallas_call(
        remote_kernel,
        in_specs=[VMEM] * 2,
        out_specs=VMEM,
        out_shape=jax.ShapeDtypeStruct((rows + 16 * (rows // hd), hd), BF),
        compiler_params=params(),
        name="attend_remote",
    )(q, kv)


def local_kernel(c_ref, q_ref, own_ref, other_ref, kv_ref, text_ref, out_ref):
    rows, hd = own_ref.shape[1:]
    head = pl.ds(pl.multiple_of(c_ref[0] * hd, hd), hd)
    core, chip, chips = c_ref[0], c_ref[1], kv_ref.shape[0] // 2
    out_ref[...] = block_sums(q_ref[...], text_ref[0, :, head], text_ref[1, :, head])
    for j in range(1, chips):
        there = pl.ds(2 * lax.rem(chip + j, chips), 2)
        k, v = (kv_ref[there, part].reshape(-1, hd) for part in (0, 1))
        out_ref[...] += block_sums(q_ref[...], k, v)
    for i, fresh in enumerate((own_ref.at[1:3], other_ref.at[1:3])):
        at = pl.ds(i * rows, rows)
        beside = 2 * chip + (1 - core if i == 0 else core)
        k, v = (jnp.concatenate([fresh[j], kv_ref[beside, j]], 0) for j in (0, 1))
        out_ref[at, :] += block_sums(q_ref[at, :], k, v)


def attend_local(core, q, own, other, kv, text):
    rows, hd = q.shape
    return pl.pallas_call(
        local_kernel,
        in_specs=[SMEM] + [VMEM] * 5,
        out_specs=VMEM,
        out_shape=jax.ShapeDtypeStruct((rows, 2 * hd), F32),
        compiler_params=params(),
        name="attend_local",
    )(core, q, own, other, kv, text)


def combine_kernel(local_ref, p1_ref, p2_ref, p3_ref, _, own_ref, other_ref):
    rows, hd = local_ref.shape[0], own_ref.shape[1]
    same = eye(hd)
    for i in range(rows // hd):
        at = slice(i * hd, (i + 1) * hd)
        summed = local_ref[at, :hd]
        totals = local_ref[at, hd:]
        line = None
        for p in (p1_ref, p2_ref, p3_ref):
            summed += p[at, :].astype(F32)
            pair = p[pl.ds(rows + 16 * i, 16), :].astype(F32)
            both = pair[0:1] + pair[8:9]
            line = both if line is None else line + both
        column = jnp.sum(jnp.broadcast_to(line, (hd, hd)) * same, 1, keepdims=True)
        done = (summed / (totals + column)).astype(BF)
        half = rows // 2
        for out_ref, start in ((own_ref, 0), (other_ref, half)):
            low, high = max(i * hd, start), min((i + 1) * hd, start + half)
            if low < high:
                out_ref[low - start : high - start, :] = done[low - i * hd : high - i * hd]


def combine(local, parts, awaited):
    rows, hd = local.shape[0], local.shape[1] // 2
    return pl.pallas_call(
        combine_kernel,
        in_specs=[VMEM] * 4 + [ANY],
        out_specs=[VMEM] * 2,
        out_shape=[jax.ShapeDtypeStruct((rows // 2, hd), BF)] * 2,
        compiler_params=params(),
        name="combine",
    )(local, *parts, awaited)


def terms_kernel(c_ref, kept_ref, swapped_ref, w_ref, out_ref, heads):
    n, _, columns = out_ref.shape
    hd = kept_ref.shape[1]
    first = c_ref[0] == 0
    heads[:, :hd] = jnp.where(first, kept_ref[...], swapped_ref[...])
    heads[:, hd:] = jnp.where(first, swapped_ref[...], kept_ref[...])
    for i in range(n):
        at = slice(i * columns, (i + 1) * columns)
        out_ref[i] = jnp.dot(heads[...], w_ref[:, at], preferred_element_type=F32).astype(BF)


def terms_of(core, kept, swapped, weight, n):
    rows, hd = kept.shape
    return pl.pallas_call(
        terms_kernel,
        in_specs=[SMEM] + [VMEM] * 3,
        out_specs=VMEM,
        out_shape=jax.ShapeDtypeStruct((n, rows, weight.shape[1] // n), BF),
        scratch_shapes=[pltpu.VMEM((rows, weight.shape[0]), BF)],
        compiler_params=params(),
        name="terms_of",
    )(core, kept, swapped, weight)


def edge_kernel(t_ref, w_ref, image_ref, gate_ref, bias_ref, _, w_out_ref, rows_ref, gate_out_ref, bias_out_ref, sems):
    columns = rows_ref.shape[1]
    mine = pl.ds(pl.multiple_of(t_ref[0] * columns, columns), columns)
    pairs = [(ref.at[:, mine], out) for ref, out in ((image_ref, rows_ref), (gate_ref, gate_out_ref), (bias_ref, bias_out_ref))]
    for copy in fetch(pairs + [(w_ref, w_out_ref)], sems):
        copy.wait()


def edge(tp, weight, image, gate, bias, n, awaited):
    rows, columns = image.shape[0], image.shape[1] // n
    return pl.pallas_call(
        edge_kernel,
        in_specs=[SMEM, HBM] + [ANY] * 4,
        out_specs=[VMEM] * 4,
        out_shape=[
            jax.ShapeDtypeStruct(weight.shape, BF),
            jax.ShapeDtypeStruct((rows, columns), BF),
            jax.ShapeDtypeStruct((1, columns), F32),
            jax.ShapeDtypeStruct((1, columns), F32),
        ],
        scratch_shapes=[pltpu.SemaphoreType.DMA((4,))],
        compiler_params=params(),
        name="edge",
    )(tp, in_hbm(weight), image, gate, bias, awaited)


def mix_kernel(terms_ref, image_ref, gate_ref, bias_ref, out_ref):
    n, rows, _ = terms_ref.shape
    step = rows // 4
    for k in range(4):
        at = pl.ds(k * step, step)
        projection = terms_ref[0, at, :].astype(F32)
        for i in range(1, n):
            projection += terms_ref[i, at, :].astype(F32)
        projection += bias_ref[...]
        piece = (image_ref[at, :].astype(F32) + gate_ref[...] * projection).astype(BF)
        for i in range(n):
            out_ref[i, at, :] = piece


def mix(terms, image, gate, bias):
    n, rows, columns = terms.shape
    return pl.pallas_call(
        mix_kernel,
        in_specs=[VMEM] * 4,
        out_specs=VMEM,
        out_shape=jax.ShapeDtypeStruct((n, rows, columns), BF),
        compiler_params=params(),
        name="mix",
    )(terms, image, gate, bias)


def join_kernel(pieces_ref, out_ref, sems):
    n, _, columns = pieces_ref.shape
    copies = fetch([(pieces_ref.at[i], out_ref.at[:, pl.ds(i * columns, columns)]) for i in range(n)], sems)
    for copy in copies:
        copy.wait()


def join(pieces):
    n, rows, columns = pieces.shape
    return pl.pallas_call(
        join_kernel,
        in_specs=[ANY],
        out_specs=HBM,
        out_shape=jax.ShapeDtypeStruct((rows, n * columns), BF),
        scratch_shapes=[pltpu.SemaphoreType.DMA((n,))],
        compiler_params=params(),
        name="join",
    )(pieces)


def shards(image, mod_shift, mod_scale, mod_gate, qkv_weight, qkv_bias, q_gain, k_gain, stale_kv, text_kv, out_weight, out_bias):
    hd = q_gain.shape[0]
    rows, features = image.shape
    n_patch = lax.axis_size("patch")
    n_tp = lax.axis_size("tp")
    patch = lax.axis_index("patch")
    tp = lax.axis_index("tp")
    core = patch % 2
    chip = (patch // 16) * 2 + (patch // 2) % 2
    core_at = jnp.stack([core, chip]).astype(jnp.int32)
    tp_at = tp.astype(jnp.int32).reshape(1)

    def flip(bits):
        return [(i, i ^ bits) for i in range(n_patch)]

    def turn(k):
        return [(i, (i & ~14) | ((i + 2 * k) & 14)) for i in range(n_patch)]

    across = [(i, (i & ~14) | ((i + (6 if i & 2 else -6)) & 14)) for i in range(n_patch)]

    def send(x, perm):
        return lax.ppermute(x, "patch", perm)

    groups = [[i | y | z | c for y in (0, 16) for z in (0, 2) for c in (0, 1)] for i in range(n_patch) if not i & 19]
    copies = copies_of(stale_kv, len(groups[0]), hd)
    kv = lax.all_to_all(copies, "patch", 0, 0, axis_index_groups=groups)

    modulated, weight = modulate(image, mod_shift, mod_scale, jnp.transpose(qkv_weight, (1, 0, 2)), copies)
    gains = (q_gain.reshape(1, -1), k_gain.reshape(1, -1))
    fresh_kv, own, away = project(core_at, modulated, weight, qkv_bias, *gains)
    other = send(away, flip(1))
    q = jnp.concatenate([own[0], other[0]], 0)

    partial = []
    for there, back in ((across, across), (turn(2), turn(6)), (turn(6), turn(2))):
        partial.append(send(attend_remote(send(q, there), kv), back))
    local = attend_local(core_at, q, own, other, kv, text_kv)
    near_weight, *rim = edge(tp_at, out_weight, image, mod_gate.reshape(1, -1), out_bias.reshape(1, -1), n_tp, local)
    kept, leaving = combine(local, partial, near_weight)

    terms = terms_of(core_at, kept, send(leaving, flip(1)), near_weight, n_tp)
    terms = lax.all_to_all(terms, "tp", 0, 0)
    pieces = mix(terms, *rim)
    mixed = join(lax.all_to_all(pieces, "tp", 0, 0))
    return (mixed, fresh_kv)


def solution(mesh):
    placed = (
        P("patch", None),
        P(),
        P(),
        P(),
        P(None, None, "tp"),
        P(None, "tp"),
        P(),
        P(),
        P(None, "patch", "tp"),
        P(None, None, "tp"),
        P("tp", None),
        P(),
    )
    return jax.shard_map(
        shards,
        mesh=mesh,
        in_specs=placed,
        out_specs=(P("patch", None), P(None, "patch", "tp")),
        check_vma=False,
    )
```

```python
import math

import jax
import jax.numpy as jnp
from jax import lax
from jax.experimental import pallas as pl
from jax.experimental.pallas import tpu as pltpu
from jax.sharding import PartitionSpec as P

BF = jnp.bfloat16
F32 = jnp.float32
VMEM = pl.BlockSpec(memory_space=pltpu.VMEM)
SMEM = pl.BlockSpec(memory_space=pltpu.SMEM)
HBM = pl.BlockSpec(memory_space=pltpu.HBM)
ANY = pl.BlockSpec(memory_space=pl.ANY)
LIMIT = 16 * 1024 * 1024


def params(**kw):
    return pltpu.CompilerParams(vmem_limit_bytes=LIMIT, **kw)


def in_hbm(x):
    return pltpu.with_memory_space_constraint(x, pltpu.HBM)


def fetch(pairs, sems):
    copies = [pltpu.make_async_copy(src, dst, sems.at[i]) for i, (src, dst) in enumerate(pairs)]
    for copy in copies:
        copy.start()
    return copies


def copies_kernel(stale_ref, out_ref, held, sems):
    n, _, _, hd = out_ref.shape
    heads = stale_ref.shape[2] // hd
    for copy in fetch([(stale_ref.at[:, :, pl.ds(i * hd, hd)], held.at[i]) for i in range(heads)], sems):
        copy.wait()
    copies = fetch([(held.at[i % heads], out_ref.at[i]) for i in range(n)], sems)
    for copy in copies:
        copy.wait()


def copies_of(stale, n, hd):
    return pl.pallas_call(
        copies_kernel,
        in_specs=[HBM],
        out_specs=HBM,
        out_shape=jax.ShapeDtypeStruct((n,) + stale.shape[:2] + (hd,), BF),
        scratch_shapes=[
            pltpu.VMEM((stale.shape[2] // hd,) + stale.shape[:2] + (hd,), BF),
            pltpu.SemaphoreType.DMA((n,)),
        ],
        compiler_params=params(),
        name="copies_of",
    )(in_hbm(stale))


def modulate_kernel(image_ref, shift_ref, scale_ref, w_ref, _, mod_ref, near_ref, image, shift, scale, sems):
    brought = pltpu.make_async_copy(w_ref, near_ref, sems.at[6])
    copies = fetch([(shift_ref, shift), (scale_ref, scale)], sems)
    rows = image_ref.shape[0]
    parts = 4
    part = rows // parts
    blocks = [
        pltpu.make_async_copy(image_ref.at[pl.ds(j * part, part)], image.at[pl.ds(j * part, part)], sems.at[2 + j])
        for j in range(parts)
    ]
    for copy in blocks:
        copy.start()
    brought.start()
    for copy in copies:
        copy.wait()
    gain = 1.0 + scale[...].reshape(1, -1)
    lift = shift[...].reshape(1, -1)
    step = 16
    for j in range(parts):
        blocks[j].wait()
        for i in range(j * part // step, (j + 1) * part // step):
            at = slice(i * step, (i + 1) * step)
            wide = image[at, :].astype(F32)
            average = jnp.mean(wide, -1, keepdims=True)
            centred = wide - average
            spread = jnp.mean(centred * centred, -1, keepdims=True)
            normed = centred * lax.rsqrt(spread + 1e-06)
            mod_ref[at, :] = (normed * gain + lift).astype(BF)
    brought.wait()


def modulate(image, shift, scale, weight, awaited):
    return pl.pallas_call(
        modulate_kernel,
        in_specs=[ANY] * 3 + [HBM, ANY],
        out_specs=[VMEM] * 2,
        out_shape=[jax.ShapeDtypeStruct(image.shape, BF), jax.ShapeDtypeStruct(weight.shape, BF)],
        scratch_shapes=[
            pltpu.VMEM(image.shape, BF),
            pltpu.VMEM(shift.shape, F32),
            pltpu.VMEM(scale.shape, F32),
            pltpu.SemaphoreType.DMA((7,)),
        ],
        compiler_params=params(),
        name="modulate",
    )(image, shift, scale, in_hbm(weight), awaited)


def finish_kernel(c_ref, sums_ref, bias_ref, q_gain_ref, k_gain_ref, fresh_ref, home_ref, away_ref):
    hd = q_gain_ref.shape[1]
    first = c_ref[0] == 0

    def norm(part, gain):
        return part * lax.rsqrt(jnp.mean(part * part, -1, keepdims=True) + 1e-06) * gain

    for j, gain_ref in enumerate((q_gain_ref, k_gain_ref, None)):
        pair = []
        for at in (slice(0, hd), slice(hd, 2 * hd)):
            part = sums_ref[j, :, at] + bias_ref[j : j + 1, at]
            pair.append((part if gain_ref is None else norm(part, gain_ref[...])).astype(BF))
            if j > 0:
                fresh_ref[j - 1, :, at] = pair[-1]
        home_ref[j] = jnp.where(first, pair[0], pair[1])
        away_ref[j] = jnp.where(first, pair[1], pair[0])


def project(core, modulated, weight, bias, q_gain, k_gain):
    rows, features = modulated.shape
    hd = q_gain.shape[1]
    sums = jnp.einsum("tf,jfc->jtc", modulated, weight, preferred_element_type=F32)
    part = jax.ShapeDtypeStruct((3, rows, hd), BF)
    return pl.pallas_call(
        finish_kernel,
        in_specs=[SMEM] + [VMEM] * 4,
        out_specs=[VMEM] * 3,
        out_shape=[jax.ShapeDtypeStruct((2, rows, weight.shape[2]), BF), part, part],
        compiler_params=params(),
        name="finish",
    )(core, sums, bias, q_gain, k_gain)


def block_sums(q, k, v_ref_value):
    hd = q.shape[1]
    scores = lax.dot_general(q, k, (((1,), (1,)), ((), ())), preferred_element_type=F32)
    weights = jnp.exp2(scores * (math.log2(math.e) / math.sqrt(hd))).astype(BF)
    ones = jnp.ones_like(v_ref_value)
    return jnp.dot(weights, jnp.concatenate([v_ref_value, ones], 1), preferred_element_type=F32)


def eye(n):
    return (lax.broadcasted_iota(jnp.int32, (n, n), 0) == lax.broadcasted_iota(jnp.int32, (n, n), 1)).astype(F32)


def remote_kernel(q_ref, kv_ref, out_ref):
    rows, hd = q_ref.shape
    same = eye(hd)
    k, v = (kv_ref[:, part].reshape(-1, hd) for part in (0, 1))
    total = block_sums(q_ref[...], k, v)
    out_ref[pl.ds(0, rows), :] = total[:, :hd].astype(BF)
    for i in range(rows // hd):
        line = jnp.sum(total[i * hd : (i + 1) * hd, hd:] * same, 0, keepdims=True)
        high = line.astype(BF).astype(F32)
        out_ref[pl.ds(rows + 16 * i, 16), :] = jnp.concatenate(
            [jnp.broadcast_to(high, (8, hd)), jnp.broadcast_to(line - high, (8, hd))], 0
        ).astype(BF)


def attend_remote(q, kv):
    rows, hd = q.shape
    return pl.pallas_call(
        remote_kernel,
        in_specs=[VMEM] * 2,
        out_specs=VMEM,
        out_shape=jax.ShapeDtypeStruct((rows + 16 * (rows // hd), hd), BF),
        compiler_params=params(),
        name="attend_remote",
    )(q, kv)


def local_kernel(c_ref, q_ref, own_ref, other_ref, kv_ref, text_ref, out_ref):
    rows, hd = own_ref.shape[1:]
    head = pl.ds(pl.multiple_of(c_ref[0] * hd, hd), hd)
    core, chip, chips = c_ref[0], c_ref[1], kv_ref.shape[0] // 2
    out_ref[...] = block_sums(q_ref[...], text_ref[0, :, head], text_ref[1, :, head])
    for j in range(1, chips):
        there = pl.ds(2 * lax.rem(chip + j, chips), 2)
        k, v = (kv_ref[there, part].reshape(-1, hd) for part in (0, 1))
        out_ref[...] += block_sums(q_ref[...], k, v)
    for i, fresh in enumerate((own_ref.at[1:3], other_ref.at[1:3])):
        at = pl.ds(i * rows, rows)
        beside = 2 * chip + (1 - core if i == 0 else core)
        k, v = (jnp.concatenate([fresh[j], kv_ref[beside, j]], 0) for j in (0, 1))
        out_ref[at, :] += block_sums(q_ref[at, :], k, v)


def attend_local(core, q, own, other, kv, text):
    rows, hd = q.shape
    return pl.pallas_call(
        local_kernel,
        in_specs=[SMEM] + [VMEM] * 5,
        out_specs=VMEM,
        out_shape=jax.ShapeDtypeStruct((rows, 2 * hd), F32),
        compiler_params=params(),
        name="attend_local",
    )(core, q, own, other, kv, text)


def combine_kernel(local_ref, p1_ref, p2_ref, p3_ref, _, own_ref, other_ref):
    rows, hd = local_ref.shape[0], own_ref.shape[1]
    same = eye(hd)
    for i in range(rows // hd):
        at = slice(i * hd, (i + 1) * hd)
        summed = local_ref[at, :hd]
        totals = local_ref[at, hd:]
        line = None
        for p in (p1_ref, p2_ref, p3_ref):
            summed += p[at, :].astype(F32)
            pair = p[pl.ds(rows + 16 * i, 16), :].astype(F32)
            both = pair[0:1] + pair[8:9]
            line = both if line is None else line + both
        column = jnp.sum(jnp.broadcast_to(line, (hd, hd)) * same, 1, keepdims=True)
        done = (summed / (totals + column)).astype(BF)
        half = rows // 2
        for out_ref, start in ((own_ref, 0), (other_ref, half)):
            low, high = max(i * hd, start), min((i + 1) * hd, start + half)
            if low < high:
                out_ref[low - start : high - start, :] = done[low - i * hd : high - i * hd]


def combine(local, parts, awaited):
    rows, hd = local.shape[0], local.shape[1] // 2
    return pl.pallas_call(
        combine_kernel,
        in_specs=[VMEM] * 4 + [ANY],
        out_specs=[VMEM] * 2,
        out_shape=[jax.ShapeDtypeStruct((rows // 2, hd), BF)] * 2,
        compiler_params=params(),
        name="combine",
    )(local, *parts, awaited)


def terms_kernel(c_ref, kept_ref, swapped_ref, w_ref, out_ref, heads):
    n, _, columns = out_ref.shape
    hd = kept_ref.shape[1]
    first = c_ref[0] == 0
    heads[:, :hd] = jnp.where(first, kept_ref[...], swapped_ref[...])
    heads[:, hd:] = jnp.where(first, swapped_ref[...], kept_ref[...])
    for i in range(n):
        at = slice(i * columns, (i + 1) * columns)
        out_ref[i] = jnp.dot(heads[...], w_ref[:, at], preferred_element_type=F32).astype(BF)


def terms_of(core, kept, swapped, weight, n):
    rows, hd = kept.shape
    return pl.pallas_call(
        terms_kernel,
        in_specs=[SMEM] + [VMEM] * 3,
        out_specs=VMEM,
        out_shape=jax.ShapeDtypeStruct((n, rows, weight.shape[1] // n), BF),
        scratch_shapes=[pltpu.VMEM((rows, weight.shape[0]), BF)],
        compiler_params=params(),
        name="terms_of",
    )(core, kept, swapped, weight)


def edge_kernel(t_ref, w_ref, image_ref, gate_ref, bias_ref, _, w_out_ref, rows_ref, gate_out_ref, bias_out_ref, sems):
    columns = rows_ref.shape[1]
    mine = pl.ds(pl.multiple_of(t_ref[0] * columns, columns), columns)
    pairs = [(ref.at[:, mine], out) for ref, out in ((image_ref, rows_ref), (gate_ref, gate_out_ref), (bias_ref, bias_out_ref))]
    for copy in fetch(pairs + [(w_ref, w_out_ref)], sems):
        copy.wait()


def edge(tp, weight, image, gate, bias, n, awaited):
    rows, columns = image.shape[0], image.shape[1] // n
    return pl.pallas_call(
        edge_kernel,
        in_specs=[SMEM, HBM] + [ANY] * 4,
        out_specs=[VMEM] * 4,
        out_shape=[
            jax.ShapeDtypeStruct(weight.shape, BF),
            jax.ShapeDtypeStruct((rows, columns), BF),
            jax.ShapeDtypeStruct((1, columns), F32),
            jax.ShapeDtypeStruct((1, columns), F32),
        ],
        scratch_shapes=[pltpu.SemaphoreType.DMA((4,))],
        compiler_params=params(),
        name="edge",
    )(tp, in_hbm(weight), image, gate, bias, awaited)


def mix_kernel(terms_ref, image_ref, gate_ref, bias_ref, out_ref):
    n, rows, _ = terms_ref.shape
    step = rows // 4
    for k in range(4):
        at = pl.ds(k * step, step)
        projection = terms_ref[0, at, :].astype(F32)
        for i in range(1, n):
            projection += terms_ref[i, at, :].astype(F32)
        projection += bias_ref[...]
        piece = (image_ref[at, :].astype(F32) + gate_ref[...] * projection).astype(BF)
        for i in range(n):
            out_ref[i, at, :] = piece


def mix(terms, image, gate, bias):
    n, rows, columns = terms.shape
    return pl.pallas_call(
        mix_kernel,
        in_specs=[VMEM] * 4,
        out_specs=VMEM,
        out_shape=jax.ShapeDtypeStruct((n, rows, columns), BF),
        compiler_params=params(),
        name="mix",
    )(terms, image, gate, bias)


def join_kernel(pieces_ref, out_ref, sems):
    n, _, columns = pieces_ref.shape
    copies = fetch([(pieces_ref.at[i], out_ref.at[:, pl.ds(i * columns, columns)]) for i in range(n)], sems)
    for copy in copies:
        copy.wait()


def join(pieces):
    n, rows, columns = pieces.shape
    return pl.pallas_call(
        join_kernel,
        in_specs=[ANY],
        out_specs=HBM,
        out_shape=jax.ShapeDtypeStruct((rows, n * columns), BF),
        scratch_shapes=[pltpu.SemaphoreType.DMA((n,))],
        compiler_params=params(),
        name="join",
    )(pieces)


def shards(image, mod_shift, mod_scale, mod_gate, qkv_weight, qkv_bias, q_gain, k_gain, stale_kv, text_kv, out_weight, out_bias):
    hd = q_gain.shape[0]
    rows, features = image.shape
    n_patch = lax.axis_size("patch")
    n_tp = lax.axis_size("tp")
    patch = lax.axis_index("patch")
    tp = lax.axis_index("tp")
    core = patch % 2
    chip = (patch // 16) * 2 + (patch // 2) % 2
    core_at = jnp.stack([core, chip]).astype(jnp.int32)
    tp_at = tp.astype(jnp.int32).reshape(1)

    def flip(bits):
        return [(i, i ^ bits) for i in range(n_patch)]

    def swap(of):
        return [(i, (i & ~14) | (of(i >> 1 & 7) % 8 << 1)) for i in range(n_patch)]

    swaps = [swap(lambda z: z + 3 if z % 2 else z - 3), swap(lambda z: z ^ 3), swap(lambda z: (z + 2 ^ 3) - 2)]

    def send(x, perm):
        return lax.ppermute(x, "patch", perm)

    groups = [[i | y | z | c for y in (0, 16) for z in (0, 2) for c in (0, 1)] for i in range(n_patch) if not i & 19]
    copies = copies_of(stale_kv, len(groups[0]), hd)
    kv = lax.all_to_all(copies, "patch", 0, 0, axis_index_groups=groups)

    modulated, weight = modulate(image, mod_shift, mod_scale, jnp.transpose(qkv_weight, (1, 0, 2)), copies)
    gains = (q_gain.reshape(1, -1), k_gain.reshape(1, -1))
    fresh_kv, own, away = project(core_at, modulated, weight, qkv_bias, *gains)
    other = send(away, flip(1))
    q = jnp.concatenate([own[0], other[0]], 0)

    partial = []
    for there in swaps:
        partial.append(send(attend_remote(send(q, there), kv), there))
    local = attend_local(core_at, q, own, other, kv, text_kv)
    near_weight, *rim = edge(tp_at, out_weight, image, mod_gate.reshape(1, -1), out_bias.reshape(1, -1), n_tp, local)
    kept, leaving = combine(local, partial, near_weight)

    terms = terms_of(core_at, kept, send(leaving, flip(1)), near_weight, n_tp)
    terms = lax.all_to_all(terms, "tp", 0, 0)
    pieces = mix(terms, *rim)
    mixed = join(lax.all_to_all(pieces, "tp", 0, 0))
    return (mixed, fresh_kv)


def solution(mesh):
    placed = (
        P("patch", None),
        P(),
        P(),
        P(),
        P(None, None, "tp"),
        P(None, "tp"),
        P(),
        P(),
        P(None, "patch", "tp"),
        P(None, None, "tp"),
        P("tp", None),
        P(),
    )
    return jax.shard_map(
        shards,
        mesh=mesh,
        in_specs=placed,
        out_specs=(P("patch", None), P(None, "patch", "tp")),
        check_vma=False,
    )
```

```python
import math

import jax
import jax.numpy as jnp
from jax import lax
from jax.experimental import pallas as pl
from jax.experimental.pallas import tpu as pltpu
from jax.sharding import PartitionSpec as P

BF = jnp.bfloat16
F32 = jnp.float32
VMEM = pl.BlockSpec(memory_space=pltpu.VMEM)
SMEM = pl.BlockSpec(memory_space=pltpu.SMEM)
HBM = pl.BlockSpec(memory_space=pltpu.HBM)
ANY = pl.BlockSpec(memory_space=pl.ANY)
LIMIT = 16 * 1024 * 1024


def params(**kw):
    return pltpu.CompilerParams(vmem_limit_bytes=LIMIT, **kw)


def in_hbm(x):
    return pltpu.with_memory_space_constraint(x, pltpu.HBM)


def fetch(pairs, sems):
    copies = [pltpu.make_async_copy(src, dst, sems.at[i]) for i, (src, dst) in enumerate(pairs)]
    for copy in copies:
        copy.start()
    return copies


def copies_kernel(stale_ref, out_ref, held, sems):
    n, _, _, hd = out_ref.shape
    heads = stale_ref.shape[2] // hd
    for copy in fetch([(stale_ref.at[:, :, pl.ds(i * hd, hd)], held.at[i]) for i in range(heads)], sems):
        copy.wait()
    copies = fetch([(held.at[i % heads], out_ref.at[i]) for i in range(n)], sems)
    for copy in copies:
        copy.wait()


def copies_of(stale, n, hd):
    return pl.pallas_call(
        copies_kernel,
        in_specs=[HBM],
        out_specs=HBM,
        out_shape=jax.ShapeDtypeStruct((n,) + stale.shape[:2] + (hd,), BF),
        scratch_shapes=[
            pltpu.VMEM((stale.shape[2] // hd,) + stale.shape[:2] + (hd,), BF),
            pltpu.SemaphoreType.DMA((n,)),
        ],
        compiler_params=params(),
        name="copies_of",
    )(in_hbm(stale))


def modulate_kernel(image_ref, shift_ref, scale_ref, w_ref, _, mod_ref, near_ref, image, shift, scale, sems):
    brought = pltpu.make_async_copy(w_ref, near_ref, sems.at[6])
    copies = fetch([(shift_ref, shift), (scale_ref, scale)], sems)
    rows = image_ref.shape[0]
    parts = 4
    part = rows // parts
    blocks = [
        pltpu.make_async_copy(image_ref.at[pl.ds(j * part, part)], image.at[pl.ds(j * part, part)], sems.at[2 + j])
        for j in range(parts)
    ]
    for copy in blocks:
        copy.start()
    brought.start()
    for copy in copies:
        copy.wait()
    gain = 1.0 + scale[...].reshape(1, -1)
    lift = shift[...].reshape(1, -1)
    step = 16
    for j in range(parts):
        blocks[j].wait()
        for i in range(j * part // step, (j + 1) * part // step):
            at = slice(i * step, (i + 1) * step)
            wide = image[at, :].astype(F32)
            average = jnp.mean(wide, -1, keepdims=True)
            centred = wide - average
            spread = jnp.mean(centred * centred, -1, keepdims=True)
            normed = centred * lax.rsqrt(spread + 1e-06)
            mod_ref[at, :] = (normed * gain + lift).astype(BF)
    brought.wait()


def modulate(image, shift, scale, weight, awaited):
    return pl.pallas_call(
        modulate_kernel,
        in_specs=[ANY] * 3 + [HBM, ANY],
        out_specs=[VMEM] * 2,
        out_shape=[jax.ShapeDtypeStruct(image.shape, BF), jax.ShapeDtypeStruct(weight.shape, BF)],
        scratch_shapes=[
            pltpu.VMEM(image.shape, BF),
            pltpu.VMEM(shift.shape, F32),
            pltpu.VMEM(scale.shape, F32),
            pltpu.SemaphoreType.DMA((7,)),
        ],
        compiler_params=params(),
        name="modulate",
    )(image, shift, scale, in_hbm(weight), awaited)


def finish_kernel(c_ref, sums_ref, bias_ref, q_gain_ref, k_gain_ref, fresh_ref, home_ref, away_ref):
    hd = q_gain_ref.shape[1]
    first = c_ref[0] == 0

    def norm(part, gain):
        return part * lax.rsqrt(jnp.mean(part * part, -1, keepdims=True) + 1e-06) * gain

    for j, gain_ref in enumerate((q_gain_ref, k_gain_ref, None)):
        pair = []
        for at in (slice(0, hd), slice(hd, 2 * hd)):
            part = sums_ref[j, :, at] + bias_ref[j : j + 1, at]
            pair.append((part if gain_ref is None else norm(part, gain_ref[...])).astype(BF))
            if j > 0:
                fresh_ref[j - 1, :, at] = pair[-1]
        home_ref[j] = jnp.where(first, pair[0], pair[1])
        away_ref[j] = jnp.where(first, pair[1], pair[0])


def project(core, modulated, weight, bias, q_gain, k_gain):
    rows, features = modulated.shape
    hd = q_gain.shape[1]
    sums = jnp.einsum("tf,jfc->jtc", modulated, weight, preferred_element_type=F32)
    part = jax.ShapeDtypeStruct((3, rows, hd), BF)
    return pl.pallas_call(
        finish_kernel,
        in_specs=[SMEM] + [VMEM] * 4,
        out_specs=[VMEM] * 3,
        out_shape=[jax.ShapeDtypeStruct((2, rows, weight.shape[2]), BF), part, part],
        compiler_params=params(),
        name="finish",
    )(core, sums, bias, q_gain, k_gain)


def block_sums(q, k, v_ref_value):
    hd = q.shape[1]
    scores = lax.dot_general(q, k, (((1,), (1,)), ((), ())), preferred_element_type=F32)
    weights = jnp.exp2(scores * (math.log2(math.e) / math.sqrt(hd))).astype(BF)
    ones = jnp.ones_like(v_ref_value)
    return jnp.dot(weights, jnp.concatenate([v_ref_value, ones], 1), preferred_element_type=F32)


def eye(n):
    return (lax.broadcasted_iota(jnp.int32, (n, n), 0) == lax.broadcasted_iota(jnp.int32, (n, n), 1)).astype(F32)


def remote_kernel(q_ref, kv_ref, out_ref):
    rows, hd = q_ref.shape
    same = eye(hd)
    k, v = (kv_ref[:, part].reshape(-1, hd) for part in (0, 1))
    total = block_sums(q_ref[...], k, v)
    out_ref[pl.ds(0, rows), :] = total[:, :hd].astype(BF)
    place = lax.broadcasted_iota(jnp.int32, (16, hd), 0)
    tile = jnp.zeros((16, hd), F32)
    for i in range(rows // hd):
        line = jnp.sum(total[i * hd : (i + 1) * hd, hd:] * same, 0, keepdims=True)
        high = line.astype(BF).astype(F32)
        tile = jnp.where(place == i, high, jnp.where(place == 8 + i, line - high, tile))
    out_ref[pl.ds(rows, 16), :] = tile.astype(BF)


def attend_remote(q, kv):
    rows, hd = q.shape
    return pl.pallas_call(
        remote_kernel,
        in_specs=[VMEM] * 2,
        out_specs=VMEM,
        out_shape=jax.ShapeDtypeStruct((rows + 16, hd), BF),
        compiler_params=params(),
        name="attend_remote",
    )(q, kv)


def local_kernel(c_ref, q_ref, own_ref, other_ref, kv_ref, text_ref, out_ref):
    rows, hd = own_ref.shape[1:]
    head = pl.ds(pl.multiple_of(c_ref[0] * hd, hd), hd)
    core, chip, chips = c_ref[0], c_ref[1], kv_ref.shape[0] // 2
    out_ref[...] = block_sums(q_ref[...], text_ref[0, :, head], text_ref[1, :, head])
    for j in range(1, chips):
        there = pl.ds(2 * lax.rem(chip + j, chips), 2)
        k, v = (kv_ref[there, part].reshape(-1, hd) for part in (0, 1))
        out_ref[...] += block_sums(q_ref[...], k, v)
    for i, fresh in enumerate((own_ref.at[1:3], other_ref.at[1:3])):
        at = pl.ds(i * rows, rows)
        beside = 2 * chip + (1 - core if i == 0 else core)
        k, v = (jnp.concatenate([fresh[j], kv_ref[beside, j]], 0) for j in (0, 1))
        out_ref[at, :] += block_sums(q_ref[at, :], k, v)


def attend_local(core, q, own, other, kv, text):
    rows, hd = q.shape
    return pl.pallas_call(
        local_kernel,
        in_specs=[SMEM] + [VMEM] * 5,
        out_specs=VMEM,
        out_shape=jax.ShapeDtypeStruct((rows, 2 * hd), F32),
        compiler_params=params(),
        name="attend_local",
    )(core, q, own, other, kv, text)


def combine_kernel(local_ref, p1_ref, p2_ref, p3_ref, _, own_ref, other_ref):
    rows, hd = local_ref.shape[0], own_ref.shape[1]
    same = eye(hd)
    for i in range(rows // hd):
        at = slice(i * hd, (i + 1) * hd)
        summed = local_ref[at, :hd]
        totals = local_ref[at, hd:]
        line = None
        for p in (p1_ref, p2_ref, p3_ref):
            summed += p[at, :].astype(F32)
            pair = p[pl.ds(rows, 16), :].astype(F32)
            both = pair[i : i + 1] + pair[8 + i : 9 + i]
            line = both if line is None else line + both
        column = jnp.sum(jnp.broadcast_to(line, (hd, hd)) * same, 1, keepdims=True)
        done = (summed / (totals + column)).astype(BF)
        half = rows // 2
        for out_ref, start in ((own_ref, 0), (other_ref, half)):
            low, high = max(i * hd, start), min((i + 1) * hd, start + half)
            if low < high:
                out_ref[low - start : high - start, :] = done[low - i * hd : high - i * hd]


def combine(local, parts, awaited):
    rows, hd = local.shape[0], local.shape[1] // 2
    return pl.pallas_call(
        combine_kernel,
        in_specs=[VMEM] * 4 + [ANY],
        out_specs=[VMEM] * 2,
        out_shape=[jax.ShapeDtypeStruct((rows // 2, hd), BF)] * 2,
        compiler_params=params(),
        name="combine",
    )(local, *parts, awaited)


def terms_kernel(c_ref, kept_ref, swapped_ref, w_ref, out_ref, heads):
    n, _, columns = out_ref.shape
    hd = kept_ref.shape[1]
    first = c_ref[0] == 0
    heads[:, :hd] = jnp.where(first, kept_ref[...], swapped_ref[...])
    heads[:, hd:] = jnp.where(first, swapped_ref[...], kept_ref[...])
    for i in range(n):
        at = slice(i * columns, (i + 1) * columns)
        out_ref[i] = jnp.dot(heads[...], w_ref[:, at], preferred_element_type=F32).astype(BF)


def terms_of(core, kept, swapped, weight, n):
    rows, hd = kept.shape
    return pl.pallas_call(
        terms_kernel,
        in_specs=[SMEM] + [VMEM] * 3,
        out_specs=VMEM,
        out_shape=jax.ShapeDtypeStruct((n, rows, weight.shape[1] // n), BF),
        scratch_shapes=[pltpu.VMEM((rows, weight.shape[0]), BF)],
        compiler_params=params(),
        name="terms_of",
    )(core, kept, swapped, weight)


def edge_kernel(t_ref, w_ref, image_ref, gate_ref, bias_ref, _, w_out_ref, rows_ref, gate_out_ref, bias_out_ref, sems):
    columns = rows_ref.shape[1]
    mine = pl.ds(pl.multiple_of(t_ref[0] * columns, columns), columns)
    pairs = [(ref.at[:, mine], out) for ref, out in ((image_ref, rows_ref), (gate_ref, gate_out_ref), (bias_ref, bias_out_ref))]
    for copy in fetch(pairs + [(w_ref, w_out_ref)], sems):
        copy.wait()


def edge(tp, weight, image, gate, bias, n, awaited):
    rows, columns = image.shape[0], image.shape[1] // n
    return pl.pallas_call(
        edge_kernel,
        in_specs=[SMEM, HBM] + [ANY] * 4,
        out_specs=[VMEM] * 4,
        out_shape=[
            jax.ShapeDtypeStruct(weight.shape, BF),
            jax.ShapeDtypeStruct((rows, columns), BF),
            jax.ShapeDtypeStruct((1, columns), F32),
            jax.ShapeDtypeStruct((1, columns), F32),
        ],
        scratch_shapes=[pltpu.SemaphoreType.DMA((4,))],
        compiler_params=params(),
        name="edge",
    )(tp, in_hbm(weight), image, gate, bias, awaited)


def mix_kernel(terms_ref, image_ref, gate_ref, bias_ref, out_ref):
    n, rows, _ = terms_ref.shape
    step = rows // 4
    for k in range(4):
        at = pl.ds(k * step, step)
        projection = terms_ref[0, at, :].astype(F32)
        for i in range(1, n):
            projection += terms_ref[i, at, :].astype(F32)
        projection += bias_ref[...]
        piece = (image_ref[at, :].astype(F32) + gate_ref[...] * projection).astype(BF)
        for i in range(n):
            out_ref[i, at, :] = piece


def mix(terms, image, gate, bias):
    n, rows, columns = terms.shape
    return pl.pallas_call(
        mix_kernel,
        in_specs=[VMEM] * 4,
        out_specs=VMEM,
        out_shape=jax.ShapeDtypeStruct((n, rows, columns), BF),
        compiler_params=params(),
        name="mix",
    )(terms, image, gate, bias)


def join_kernel(pieces_ref, out_ref, sems):
    n, _, columns = pieces_ref.shape
    copies = fetch([(pieces_ref.at[i], out_ref.at[:, pl.ds(i * columns, columns)]) for i in range(n)], sems)
    for copy in copies:
        copy.wait()


def join(pieces):
    n, rows, columns = pieces.shape
    return pl.pallas_call(
        join_kernel,
        in_specs=[ANY],
        out_specs=HBM,
        out_shape=jax.ShapeDtypeStruct((rows, n * columns), BF),
        scratch_shapes=[pltpu.SemaphoreType.DMA((n,))],
        compiler_params=params(),
        name="join",
    )(pieces)


def shards(image, mod_shift, mod_scale, mod_gate, qkv_weight, qkv_bias, q_gain, k_gain, stale_kv, text_kv, out_weight, out_bias):
    hd = q_gain.shape[0]
    rows, features = image.shape
    n_patch = lax.axis_size("patch")
    n_tp = lax.axis_size("tp")
    patch = lax.axis_index("patch")
    tp = lax.axis_index("tp")
    core = patch % 2
    chip = (patch // 16) * 2 + (patch // 2) % 2
    core_at = jnp.stack([core, chip]).astype(jnp.int32)
    tp_at = tp.astype(jnp.int32).reshape(1)

    def flip(bits):
        return [(i, i ^ bits) for i in range(n_patch)]

    def swap(of):
        return [(i, (i & ~14) | (of(i >> 1 & 7) % 8 << 1)) for i in range(n_patch)]

    swaps = [swap(lambda z: z + 3 if z % 2 else z - 3), swap(lambda z: z ^ 3), swap(lambda z: (z + 2 ^ 3) - 2)]

    def send(x, perm):
        return lax.ppermute(x, "patch", perm)

    groups = [[i | y | z | c for y in (0, 16) for z in (0, 2) for c in (0, 1)] for i in range(n_patch) if not i & 19]
    copies = copies_of(stale_kv, len(groups[0]), hd)
    kv = lax.all_to_all(copies, "patch", 0, 0, axis_index_groups=groups)

    modulated, weight = modulate(image, mod_shift, mod_scale, jnp.transpose(qkv_weight, (1, 0, 2)), copies)
    gains = (q_gain.reshape(1, -1), k_gain.reshape(1, -1))
    fresh_kv, own, away = project(core_at, modulated, weight, qkv_bias, *gains)
    other = send(away, flip(1))
    q = jnp.concatenate([own[0], other[0]], 0)

    partial = []
    for there in swaps:
        partial.append(send(attend_remote(send(q, there), kv), there))
    local = attend_local(core_at, q, own, other, kv, text_kv)
    near_weight, *rim = edge(tp_at, out_weight, image, mod_gate.reshape(1, -1), out_bias.reshape(1, -1), n_tp, local)
    kept, leaving = combine(local, partial, near_weight)

    terms = terms_of(core_at, kept, send(leaving, flip(1)), near_weight, n_tp)
    terms = lax.all_to_all(terms, "tp", 0, 0)
    pieces = mix(terms, *rim)
    mixed = join(lax.all_to_all(pieces, "tp", 0, 0))
    return (mixed, fresh_kv)


def solution(mesh):
    placed = (
        P("patch", None),
        P(),
        P(),
        P(),
        P(None, None, "tp"),
        P(None, "tp"),
        P(),
        P(),
        P(None, "patch", "tp"),
        P(None, None, "tp"),
        P("tp", None),
        P(),
    )
    return jax.shard_map(
        shards,
        mesh=mesh,
        in_specs=placed,
        out_specs=(P("patch", None), P(None, "patch", "tp")),
        check_vma=False,
    )
```

```python
import math

import jax
import jax.numpy as jnp
from jax import lax
from jax.experimental import pallas as pl
from jax.experimental.pallas import tpu as pltpu
from jax.sharding import PartitionSpec as P

BF = jnp.bfloat16
F32 = jnp.float32
VMEM = pl.BlockSpec(memory_space=pltpu.VMEM)
SMEM = pl.BlockSpec(memory_space=pltpu.SMEM)
HBM = pl.BlockSpec(memory_space=pltpu.HBM)
ANY = pl.BlockSpec(memory_space=pl.ANY)
LIMIT = 16 * 1024 * 1024


def params(**kw):
    return pltpu.CompilerParams(vmem_limit_bytes=LIMIT, **kw)


def in_hbm(x):
    return pltpu.with_memory_space_constraint(x, pltpu.HBM)


def fetch(pairs, sems):
    copies = [pltpu.make_async_copy(src, dst, sems.at[i]) for i, (src, dst) in enumerate(pairs)]
    for copy in copies:
        copy.start()
    return copies


def copies_kernel(stale_ref, out_ref, held, sems):
    n, _, _, hd = out_ref.shape
    heads = stale_ref.shape[2] // hd
    for copy in fetch([(stale_ref.at[:, :, pl.ds(i * hd, hd)], held.at[i]) for i in range(heads)], sems):
        copy.wait()
    copies = fetch([(held.at[i % heads], out_ref.at[i]) for i in range(n)], sems)
    for copy in copies:
        copy.wait()


def copies_of(stale, n, hd):
    return pl.pallas_call(
        copies_kernel,
        in_specs=[HBM],
        out_specs=HBM,
        out_shape=jax.ShapeDtypeStruct((n,) + stale.shape[:2] + (hd,), BF),
        scratch_shapes=[
            pltpu.VMEM((stale.shape[2] // hd,) + stale.shape[:2] + (hd,), BF),
            pltpu.SemaphoreType.DMA((n,)),
        ],
        compiler_params=params(),
        name="copies_of",
    )(in_hbm(stale))


def modulate_kernel(image_ref, shift_ref, scale_ref, w_ref, _, mod_ref, near_ref, image, shift, scale, sems):
    brought = pltpu.make_async_copy(w_ref, near_ref, sems.at[6])
    copies = fetch([(shift_ref, shift), (scale_ref, scale)], sems)
    rows = image_ref.shape[0]
    parts = 4
    part = rows // parts
    blocks = [
        pltpu.make_async_copy(image_ref.at[pl.ds(j * part, part)], image.at[pl.ds(j * part, part)], sems.at[2 + j])
        for j in range(parts)
    ]
    for copy in blocks:
        copy.start()
    brought.start()
    for copy in copies:
        copy.wait()
    gain = 1.0 + scale[...].reshape(1, -1)
    lift = shift[...].reshape(1, -1)
    step = 16
    for j in range(parts):
        blocks[j].wait()
        for i in range(j * part // step, (j + 1) * part // step):
            at = slice(i * step, (i + 1) * step)
            wide = image[at, :].astype(F32)
            average = jnp.mean(wide, -1, keepdims=True)
            centred = wide - average
            spread = jnp.mean(centred * centred, -1, keepdims=True)
            normed = centred * lax.rsqrt(spread + 1e-06)
            mod_ref[at, :] = (normed * gain + lift).astype(BF)
    brought.wait()


def modulate(image, shift, scale, weight, awaited):
    return pl.pallas_call(
        modulate_kernel,
        in_specs=[ANY] * 3 + [HBM, ANY],
        out_specs=[VMEM] * 2,
        out_shape=[jax.ShapeDtypeStruct(image.shape, BF), jax.ShapeDtypeStruct(weight.shape, BF)],
        scratch_shapes=[
            pltpu.VMEM(image.shape, BF),
            pltpu.VMEM(shift.shape, F32),
            pltpu.VMEM(scale.shape, F32),
            pltpu.SemaphoreType.DMA((7,)),
        ],
        compiler_params=params(),
        name="modulate",
    )(image, shift, scale, in_hbm(weight), awaited)


def finish_kernel(c_ref, sums_ref, bias_ref, q_gain_ref, k_gain_ref, fresh_ref, home_ref, away_ref):
    hd = q_gain_ref.shape[1]
    first = c_ref[0] == 0

    def norm(part, gain):
        return part * lax.rsqrt(jnp.mean(part * part, -1, keepdims=True) + 1e-06) * gain

    for j, gain_ref in enumerate((q_gain_ref, k_gain_ref, None)):
        pair = []
        for at in (slice(0, hd), slice(hd, 2 * hd)):
            part = sums_ref[j, :, at] + bias_ref[j : j + 1, at]
            pair.append((part if gain_ref is None else norm(part, gain_ref[...])).astype(BF))
            if j > 0:
                fresh_ref[j - 1, :, at] = pair[-1]
        home_ref[j] = jnp.where(first, pair[0], pair[1])
        away_ref[j] = jnp.where(first, pair[1], pair[0])


def project(core, modulated, weight, bias, q_gain, k_gain):
    rows, features = modulated.shape
    hd = q_gain.shape[1]
    sums = jnp.einsum("tf,jfc->jtc", modulated, weight, preferred_element_type=F32)
    part = jax.ShapeDtypeStruct((3, rows, hd), BF)
    return pl.pallas_call(
        finish_kernel,
        in_specs=[SMEM] + [VMEM] * 4,
        out_specs=[VMEM] * 3,
        out_shape=[jax.ShapeDtypeStruct((2, rows, weight.shape[2]), BF), part, part],
        compiler_params=params(),
        name="finish",
    )(core, sums, bias, q_gain, k_gain)


def block_sums(q, k, v_ref_value):
    hd = q.shape[1]
    scores = lax.dot_general(q, k, (((1,), (1,)), ((), ())), preferred_element_type=F32)
    weights = jnp.exp2(scores * (math.log2(math.e) / math.sqrt(hd))).astype(BF)
    ones = jnp.ones_like(v_ref_value)
    return jnp.dot(weights, jnp.concatenate([v_ref_value, ones], 1), preferred_element_type=F32)


def eye(n):
    return (lax.broadcasted_iota(jnp.int32, (n, n), 0) == lax.broadcasted_iota(jnp.int32, (n, n), 1)).astype(F32)


def remote_kernel(q_ref, kv_ref, out_ref):
    rows, hd = q_ref.shape
    same = eye(hd)
    k, v = (kv_ref[:, part].reshape(-1, hd) for part in (0, 1))
    total = block_sums(q_ref[...], k, v)
    out_ref[pl.ds(0, rows), :] = total[:, :hd].astype(BF)
    place = lax.broadcasted_iota(jnp.int32, (16, hd), 0)
    tile = jnp.zeros((16, hd), F32)
    for i in range(rows // hd):
        line = jnp.sum(total[i * hd : (i + 1) * hd, hd:] * same, 0, keepdims=True)
        high = line.astype(BF).astype(F32)
        tile = jnp.where(place == i, high, jnp.where(place == 8 + i, line - high, tile))
    out_ref[pl.ds(rows, 16), :] = tile.astype(BF)


def attend_remote(q, kv):
    rows, hd = q.shape
    return pl.pallas_call(
        remote_kernel,
        in_specs=[VMEM] * 2,
        out_specs=VMEM,
        out_shape=jax.ShapeDtypeStruct((rows + 16, hd), BF),
        compiler_params=params(),
        name="attend_remote",
    )(q, kv)


def local_kernel(c_ref, q_ref, own_ref, other_ref, kv_ref, text_ref, out_ref):
    rows, hd = own_ref.shape[1:]
    head = pl.ds(pl.multiple_of(c_ref[0] * hd, hd), hd)
    core, chip, chips = c_ref[0], c_ref[1], kv_ref.shape[0] // 2
    out_ref[...] = block_sums(q_ref[...], text_ref[0, :, head], text_ref[1, :, head])
    for j in range(1, chips):
        there = pl.ds(2 * lax.rem(chip + j, chips), 2)
        k, v = (kv_ref[there, part].reshape(-1, hd) for part in (0, 1))
        out_ref[...] += block_sums(q_ref[...], k, v)
    for i, fresh in enumerate((own_ref.at[1:3], other_ref.at[1:3])):
        at = pl.ds(i * rows, rows)
        beside = 2 * chip + (1 - core if i == 0 else core)
        k, v = (jnp.concatenate([fresh[j], kv_ref[beside, j]], 0) for j in (0, 1))
        out_ref[at, :] += block_sums(q_ref[at, :], k, v)


def attend_local(core, q, own, other, kv, text):
    rows, hd = q.shape
    return pl.pallas_call(
        local_kernel,
        in_specs=[SMEM] + [VMEM] * 5,
        out_specs=VMEM,
        out_shape=jax.ShapeDtypeStruct((rows, 2 * hd), F32),
        compiler_params=params(),
        name="attend_local",
    )(core, q, own, other, kv, text)


def combine_kernel(local_ref, p1_ref, p2_ref, p3_ref, _, own_ref, other_ref):
    rows, hd = local_ref.shape[0], own_ref.shape[1]
    same = eye(hd)
    for i in range(rows // hd):
        at = slice(i * hd, (i + 1) * hd)
        summed = local_ref[at, :hd]
        totals = local_ref[at, hd:]
        line = None
        for p in (p1_ref, p2_ref, p3_ref):
            summed += p[at, :].astype(F32)
            pair = p[pl.ds(rows, 16), :].astype(F32)
            both = pair[i : i + 1] + pair[8 + i : 9 + i]
            line = both if line is None else line + both
        column = jnp.sum(jnp.broadcast_to(line, (hd, hd)) * same, 1, keepdims=True)
        done = (summed / (totals + column)).astype(BF)
        half = rows // 2
        for out_ref, start in ((own_ref, 0), (other_ref, half)):
            low, high = max(i * hd, start), min((i + 1) * hd, start + half)
            if low < high:
                out_ref[low - start : high - start, :] = done[low - i * hd : high - i * hd]


def combine(local, parts, awaited):
    rows, hd = local.shape[0], local.shape[1] // 2
    return pl.pallas_call(
        combine_kernel,
        in_specs=[VMEM] * 4 + [ANY],
        out_specs=[VMEM] * 2,
        out_shape=[jax.ShapeDtypeStruct((rows // 2, hd), BF)] * 2,
        compiler_params=params(),
        name="combine",
    )(local, *parts, awaited)


def terms_kernel(c_ref, kept_ref, swapped_ref, w_ref, out_ref, heads):
    n, _, columns = out_ref.shape
    hd = kept_ref.shape[1]
    first = c_ref[0] == 0
    heads[:, :hd] = jnp.where(first, kept_ref[...], swapped_ref[...])
    heads[:, hd:] = jnp.where(first, swapped_ref[...], kept_ref[...])
    for i in range(n):
        at = slice(i * columns, (i + 1) * columns)
        out_ref[i] = jnp.dot(heads[...], w_ref[:, at], preferred_element_type=F32).astype(BF)


def terms_of(core, kept, swapped, weight, n):
    rows, hd = kept.shape
    return pl.pallas_call(
        terms_kernel,
        in_specs=[SMEM] + [VMEM] * 3,
        out_specs=VMEM,
        out_shape=jax.ShapeDtypeStruct((n, rows, weight.shape[1] // n), BF),
        scratch_shapes=[pltpu.VMEM((rows, weight.shape[0]), BF)],
        compiler_params=params(),
        name="terms_of",
    )(core, kept, swapped, weight)


def edge_kernel(t_ref, w_ref, image_ref, gate_ref, bias_ref, _, w_out_ref, rows_ref, gate_out_ref, bias_out_ref, sems):
    columns = rows_ref.shape[1]
    mine = pl.ds(pl.multiple_of(t_ref[0] * columns, columns), columns)
    pairs = [(ref.at[:, mine], out) for ref, out in ((image_ref, rows_ref), (gate_ref, gate_out_ref), (bias_ref, bias_out_ref))]
    for copy in fetch(pairs + [(w_ref, w_out_ref)], sems):
        copy.wait()


def edge(tp, weight, image, gate, bias, n, awaited):
    rows, columns = image.shape[0], image.shape[1] // n
    return pl.pallas_call(
        edge_kernel,
        in_specs=[SMEM, HBM] + [ANY] * 4,
        out_specs=[VMEM] * 4,
        out_shape=[
            jax.ShapeDtypeStruct(weight.shape, BF),
            jax.ShapeDtypeStruct((rows, columns), BF),
            jax.ShapeDtypeStruct((1, columns), F32),
            jax.ShapeDtypeStruct((1, columns), F32),
        ],
        scratch_shapes=[pltpu.SemaphoreType.DMA((4,))],
        compiler_params=params(),
        name="edge",
    )(tp, in_hbm(weight), image, gate, bias, awaited)


def mix_kernel(terms_ref, image_ref, gate_ref, bias_ref, out_ref):
    n, rows, _ = terms_ref.shape
    step = rows // 4
    for k in range(4):
        at = pl.ds(k * step, step)
        projection = terms_ref[0, at, :].astype(F32)
        for i in range(1, n):
            projection += terms_ref[i, at, :].astype(F32)
        projection += bias_ref[...]
        piece = (image_ref[at, :].astype(F32) + gate_ref[...] * projection).astype(BF)
        for i in range(n):
            out_ref[i, at, :] = piece


def mix(terms, image, gate, bias):
    n, rows, columns = terms.shape
    return pl.pallas_call(
        mix_kernel,
        in_specs=[VMEM] * 4,
        out_specs=VMEM,
        out_shape=jax.ShapeDtypeStruct((n, rows, columns), BF),
        compiler_params=params(),
        name="mix",
    )(terms, image, gate, bias)


def join_kernel(pieces_ref, out_ref, sems):
    n, rows, columns = pieces_ref.shape
    pairs = []
    for at in (pl.ds(0, rows // 2), pl.ds(rows // 2, rows // 2)):
        pairs += [(pieces_ref.at[i, at], out_ref.at[at, pl.ds(i * columns, columns)]) for i in range(n)]
    copies = fetch(pairs, sems)
    for copy in copies:
        copy.wait()


def join(pieces):
    n, rows, columns = pieces.shape
    return pl.pallas_call(
        join_kernel,
        in_specs=[ANY],
        out_specs=HBM,
        out_shape=jax.ShapeDtypeStruct((rows, n * columns), BF),
        scratch_shapes=[pltpu.SemaphoreType.DMA((2 * n,))],
        compiler_params=params(),
        name="join",
    )(pieces)


def shards(image, mod_shift, mod_scale, mod_gate, qkv_weight, qkv_bias, q_gain, k_gain, stale_kv, text_kv, out_weight, out_bias):
    hd = q_gain.shape[0]
    rows, features = image.shape
    n_patch = lax.axis_size("patch")
    n_tp = lax.axis_size("tp")
    patch = lax.axis_index("patch")
    tp = lax.axis_index("tp")
    core = patch % 2
    chip = (patch // 16) * 2 + (patch // 2) % 2
    core_at = jnp.stack([core, chip]).astype(jnp.int32)
    tp_at = tp.astype(jnp.int32).reshape(1)

    def flip(bits):
        return [(i, i ^ bits) for i in range(n_patch)]

    def swap(of):
        return [(i, (i & ~14) | (of(i >> 1 & 7) % 8 << 1)) for i in range(n_patch)]

    swaps = [swap(lambda z: z + 3 if z % 2 else z - 3), swap(lambda z: z ^ 3), swap(lambda z: (z + 2 ^ 3) - 2)]

    def send(x, perm):
        return lax.ppermute(x, "patch", perm)

    groups = [[i | y | z | c for y in (0, 16) for z in (0, 2) for c in (0, 1)] for i in range(n_patch) if not i & 19]
    copies = copies_of(stale_kv, len(groups[0]), hd)
    kv = lax.all_to_all(copies, "patch", 0, 0, axis_index_groups=groups)

    modulated, weight = modulate(image, mod_shift, mod_scale, jnp.transpose(qkv_weight, (1, 0, 2)), copies)
    gains = (q_gain.reshape(1, -1), k_gain.reshape(1, -1))
    fresh_kv, own, away = project(core_at, modulated, weight, qkv_bias, *gains)
    other = send(away, flip(1))
    q = jnp.concatenate([own[0], other[0]], 0)

    partial = []
    for there in swaps:
        partial.append(send(attend_remote(send(q, there), kv), there))
    local = attend_local(core_at, q, own, other, kv, text_kv)
    near_weight, *rim = edge(tp_at, out_weight, image, mod_gate.reshape(1, -1), out_bias.reshape(1, -1), n_tp, local)
    kept, leaving = combine(local, partial, near_weight)

    terms = terms_of(core_at, kept, send(leaving, flip(1)), near_weight, n_tp)
    terms = lax.all_to_all(terms, "tp", 0, 0)
    pieces = mix(terms, *rim)
    mixed = join(lax.all_to_all(pieces, "tp", 0, 0))
    return (mixed, fresh_kv)


def solution(mesh):
    placed = (
        P("patch", None),
        P(),
        P(),
        P(),
        P(None, None, "tp"),
        P(None, "tp"),
        P(),
        P(),
        P(None, "patch", "tp"),
        P(None, None, "tp"),
        P("tp", None),
        P(),
    )
    return jax.shard_map(
        shards,
        mesh=mesh,
        in_specs=placed,
        out_specs=(P("patch", None), P(None, "patch", "tp")),
        check_vma=False,
    )
```
